32 devices in a mesh: replica: 4 (over y, x), fsdp: 4 (over z), tensor: 2 (over core).
Axes of the slice: x: 2, y: 2, z: 4, core: 2. Of those that a mesh axis runs over, the one named last changes fastest.
Arguments:
- momentum: float32 [4, 1024, 3584], P('replica', 'fsdp', 'tensor'), may hold values from -600 to 600
- gradient: bfloat16 [4, 1024, 3584], P('replica', 'fsdp', 'tensor'), may hold values from -300 to 300
- right_in: float32 [3584, 256], P(('tensor', 'fsdp')), may hold values from -6 to 6
Outputs:
- left_factor: float32 [1024, 256], P('fsdp')
- right_factor: float32 [3584, 256], P(('tensor', 'fsdp'))
- new_momentum: float32 [4, 1024, 3584], P('replica', 'fsdp', 'tensor')
The draws below stay inside these ranges and needn't reach their ends.
All inputs are finite; a program needn't handle non-finite values.
Results may differ from the reference program's by a relative error of at most 0.0003.
Values sent between devices are 32-bit elements; how exact they have to be, the bound alone decides.
A program may use at most 64 MiB of HBM per device.

```python
import math
import jax
import jax.numpy as jnp
from jax import lax

RANK = 256
REPLICAS = 4
ROWS = 1024
COLS = 3584


def scales(key, count, spread):
    levels = jnp.exp(jax.random.uniform(key, (count,), jnp.float32, -spread, spread))
    rising = jnp.sqrt(1.0 + 2.0 * jnp.arange(count, dtype=jnp.float32) / count)
    return levels * rising


def column_basis(key):
    basis_key = jax.random.fold_in(key, 97)
    return jnp.clip(jax.random.normal(basis_key, (COLS, RANK), jnp.float32), -4.0, 4.0)


def draw_momentum(key, part):
    basis = column_basis(key)
    key = jax.random.fold_in(key, 11)
    key_noise, key_rows, key_cols, key_left = jax.random.split(key, 4)
    left_part = jnp.clip(jax.random.normal(key_left, (ROWS, RANK), jnp.float32), -4.0, 4.0)
    shared = jnp.dot(left_part, basis.T, precision=lax.Precision.HIGHEST) * RANK ** (-0.5)
    shared = jnp.clip(shared, -4.0, 4.0)
    noise = jnp.clip(jax.random.normal(key_noise, (REPLICAS, ROWS, COLS), jnp.float32), -4.0, 4.0)
    row_scale = scales(key_rows, ROWS, 1.1513)
    col_scale = scales(key_cols, COLS, 1.1513)
    mixed = 2.5 * shared[None, :, :] + noise
    return mixed * row_scale[None, :, None] * col_scale[None, None, :]


def draw_gradient(key, part):
    key = jax.random.fold_in(key, 23)
    key_noise, key_rows, key_cols = jax.random.split(key, 3)
    noise = jnp.clip(jax.random.normal(key_noise, (REPLICAS, ROWS, COLS), jnp.float32), -4.0, 4.0)
    row_scale = scales(key_rows, ROWS, 1.1513)
    col_scale = scales(key_cols, COLS, 1.1513)
    return (noise * row_scale[None, :, None] * col_scale[None, None, :]).astype(jnp.bfloat16)


def draw_right_in(key, part):
    basis = column_basis(key)
    key = jax.random.fold_in(key, 37)
    extra = 0.5 * jnp.clip(jax.random.normal(key, (COLS, RANK), jnp.float32), -4.0, 4.0)
    return basis + extra


def setup_inputs(seed: int = 0) -> dict:
    key_of = jax.random.split(jax.random.key(seed), 4)
    return {
        "momentum": draw_momentum(jax.random.fold_in(key_of[3], 71), 0),
        "gradient": draw_gradient(jax.random.fold_in(key_of[3], 71), 0),
        "right_in": draw_right_in(jax.random.fold_in(key_of[3], 71), 0),
    }


def reference(momentum, gradient, right_in):
    highest = lax.Precision.HIGHEST
    projected = jnp.zeros((ROWS, RANK), jnp.float32)
    for replica_index in range(REPLICAS):
        buffer = momentum[replica_index] + gradient[replica_index].astype(jnp.float32)
        projected = projected + jnp.dot(buffer, right_in, precision=highest)
    projected = projected / REPLICAS
    gram_matrix = jnp.dot(projected.T, projected, precision=highest)
    factor_low = jnp.linalg.cholesky(gram_matrix)
    orthonormal = jax.scipy.linalg.solve_triangular(factor_low, projected.T, lower=True).T
    back_proj = jnp.zeros((COLS, RANK), jnp.float32)
    for replica_index in range(REPLICAS):
        buffer = momentum[replica_index] + gradient[replica_index].astype(jnp.float32)
        back_proj = back_proj + jnp.dot(buffer.T, orthonormal, precision=highest)
    back_proj = back_proj / REPLICAS
    column_norm = jnp.sqrt(lax.optimization_barrier(jnp.sum(back_proj * back_proj, axis=0)) + 1e-06)
    right_factor = back_proj * (math.sqrt(COLS) / column_norm)[None, :]
    left_factor = orthonormal * math.sqrt(ROWS)
    correction = 0.1 * jnp.dot(orthonormal, back_proj.T, precision=highest)
    updated = []
    for replica_index in range(REPLICAS):
        buffer = momentum[replica_index] + gradient[replica_index].astype(jnp.float32)
        updated.append(buffer - correction)
    return (left_factor, right_factor, jnp.stack(updated))
```

```python
import math

import jax
import jax.numpy as jnp
from jax import lax
from jax.experimental import pallas as pl
from jax.experimental.pallas import tpu as pltpu
from jax.sharding import PartitionSpec as P

MESH = pl.DeviceIdType.MESH
HIGHEST = lax.Precision.HIGHEST
F32 = jnp.float32


def dot(a, b, ca, cb):
    return lax.dot_general(
        a, b, (((ca,), (cb,)), ((), ())), precision=HIGHEST, preferred_element_type=F32
    )


def vmem(n):
    return [pl.BlockSpec(memory_space=pltpu.VMEM)] * n


class Place:
    def __init__(self, R, F, T):
        self.R, self.F, self.T, self.n = R, F, T, R * T
        self.r = lax.axis_index("replica")
        self.f = lax.axis_index("fsdp")
        self.t = lax.axis_index("tensor")
        self.p = self.r * T + self.t

    def plane(self, d):
        q = lax.rem(self.p + d, self.n)
        return q, {"replica": q // self.T, "tensor": lax.rem(q, self.T)}

    def plane_from(self, d):
        return lax.rem(self.p + self.n - d, self.n)

    def line(self, d):
        q = lax.rem(self.f + d, self.F)
        return q, {"fsdp": q}

    def line_from(self, d):
        return lax.rem(self.f + self.F - d, self.F)

    def rep(self, d):
        q = lax.rem(self.r + d, self.R)
        return q, {"replica": q}

    def rep_from(self, d):
        return lax.rem(self.r + self.R - d, self.R)


def remote(src, dst, send, recv, where):
    return pltpu.make_async_remote_copy(
        src_ref=src, dst_ref=dst, send_sem=send, recv_sem=recv, device_id=where, device_id_type=MESH
    )


def greet(targets):
    barrier = pltpu.get_barrier_semaphore()
    for where in targets:
        pl.semaphore_signal(barrier, inc=1, device_id=where, device_id_type=MESH)
    pl.semaphore_wait(barrier, len(targets))


def project_kernel(
    R, F, T, mom, grad, q_in, bmean_out, proj_out, gram_out,
    bufs, brecv, qs, pp, precv, proj, gp, grecv, gram,
    b_send, b_recv, q_up, q_down, q_recv, p_send, p_recv, a_send, a_recv,
    g_send, g_recv, h_send, h_recv,
):
    at = Place(R, F, T)
    rows, cols = mom.shape[1], mom.shape[2]
    share = cols // R
    n = at.n
    piece = rows // n
    for k in range(R):
        part = slice(k * share, (k + 1) * share)
        bufs[k] = mom[0, :, part] + grad[0, :, part].astype(F32)
    nb = F // R
    qb = q_in.shape[0]
    nc, qc = qs.shape[1], qs.shape[2]
    for j in range(nb):
        @pl.when(at.f == at.r * nb + j)
        def _():
            for c in range(nc):
                qs[j, c] = q_in[c * qc:(c + 1) * qc, :]

    greet([at.plane(d)[1] for d in range(1, n)] + [at.line(d)[1] for d in range(1, F)])

    sent = []
    for d in range(1, R):
        k, where = at.rep(d)
        copy = remote(bufs.at[k], brecv.at[at.r], b_send.at[d - 1], b_recv.at[at.r], where)
        copy.start()
        sent.append(copy)

    def up(j, c):
        return remote(qs.at[j, c], qs.at[j, c], q_up.at[j, c], q_recv.at[j, c], {"fsdp": lax.rem(at.f + 1, F)})

    def down(j, c):
        return remote(qs.at[j, c], qs.at[j, c], q_down.at[j, c], q_recv.at[j, c], {"fsdp": lax.rem(at.f + F - 1, F)})

    for c in range(nc):
        for j in range(nb):
            home = at.r * nb + j
            @pl.when(at.f != home)
            def _():
                up(j, c).wait_recv()
            @pl.when((at.f >= home) & (at.f < F - 1))
            def _():
                up(j, c).start()
            @pl.when((at.f <= home) & (at.f > 0))
            def _():
                down(j, c).start()

    brecv[at.r] = bufs[at.r]
    for d in range(1, R):
        k = at.rep_from(d)
        remote(bufs.at[k], brecv.at[k], b_send.at[d - 1], b_recv.at[k], at.rep(d)[1]).wait_recv()
    total = brecv[0]
    for k in range(1, R):
        total = total + brecv[k]
    bmean = total * (1.0 / R)
    bmean_out[...] = bmean
    part = dot(bmean, qs[...].reshape(share, q_in.shape[1]), 1, 0)
    pp[...] = part.reshape(pp.shape)

    for d in range(1, n):
        q, where = at.plane(d)
        copy = remote(pp.at[q], precv.at[at.p], p_send.at[d - 1], p_recv.at[at.p], where)
        copy.start()
        sent.append(copy)
    precv[at.p] = pp[at.p]
    for d in range(1, n):
        q = at.plane_from(d)
        remote(pp.at[q], precv.at[q], p_send.at[d - 1], p_recv.at[q], at.plane(d)[1]).wait_recv()
    total = precv[0]
    for k in range(1, n):
        total = total + precv[k]
    proj[at.p] = total
    for d in range(1, n):
        q, where = at.plane(d)
        copy = remote(proj.at[at.p], proj.at[at.p], a_send.at[d - 1], a_recv.at[at.p], where)
        copy.start()
        sent.append(copy)
    for d in range(1, n):
        q = at.plane_from(d)
        remote(proj.at[q], proj.at[q], a_send.at[d - 1], a_recv.at[q], at.plane(d)[1]).wait_recv()
    whole = proj[...].reshape(rows, q_in.shape[1])
    proj_out[...] = whole

    gp[...] = dot(whole, whole, 0, 0).reshape(gp.shape)
    for d in range(1, F):
        q, where = at.line(d)
        copy = remote(gp.at[at.p], grecv.at[at.f], g_send.at[d - 1], g_recv.at[at.f], where)
        copy.start()
        sent.append(copy)
    grecv[at.f] = gp[at.p]
    for d in range(1, F):
        q = at.line_from(d)
        remote(gp.at[at.p], grecv.at[q], g_send.at[d - 1], g_recv.at[q], at.line(d)[1]).wait_recv()
    total = grecv[0]
    for k in range(1, F):
        total = total + grecv[k]
    gram[at.p] = total
    for d in range(1, n):
        q, where = at.plane(d)
        copy = remote(gram.at[at.p], gram.at[at.p], h_send.at[d - 1], h_recv.at[at.p], where)
        copy.start()
        sent.append(copy)
    for d in range(1, n):
        q = at.plane_from(d)
        remote(gram.at[q], gram.at[q], h_send.at[d - 1], h_recv.at[q], at.plane(d)[1]).wait_recv()
    gram_out[...] = gram[...].reshape(gram_out.shape)

    for copy in sent:
        copy.wait_send()
    for c in range(nc):
        for j in range(nb):
            home = at.r * nb + j
            @pl.when((at.f >= home) & (at.f < F - 1))
            def _():
                up(j, c).wait_send()
            @pl.when((at.f <= home) & (at.f > 0))
            def _():
                down(j, c).wait_send()


def eliminate(tile, side):
    b = tile.shape[0]
    rows_id = lax.broadcasted_iota(jnp.int32, tile.shape, 0)
    lanes = lax.broadcasted_iota(jnp.int32, tile.shape, 1)
    other = b - side
    inside = (lanes >= side) & (lanes < side + b)
    x = jnp.where(inside, tile, jnp.where(lanes - other == rows_id, 1.0, 0.0).astype(F32))
    done = []
    for k0 in range(0, b, 8):
        shape = x.shape
        ids = lax.broadcasted_iota(jnp.int32, shape, 0)
        panel = [
            jnp.broadcast_to(x[:, side + k0 + j:side + k0 + j + 1], shape) for j in range(8)
        ]
        for j in range(8):
            inverse = 1.0 / panel[j][j:j + 1, :]
            scale = jnp.where(ids > j, panel[j], 0.0) * inverse
            for i in range(j + 1, 8):
                panel[i] = panel[i] - scale * panel[i][j:j + 1, :]
            x = x - scale * x[j:j + 1, :]
        done.append(x[:8])
        x = x[8:]
    x = jnp.concatenate(done, axis=0)
    pivot = jnp.sum(jnp.where(lanes - side == rows_id, x, 0.0), axis=1, keepdims=True)
    return x * (1.0 / jnp.sqrt(pivot))


def factor_kernel(scale, gram, proj, ortho, left, w):
    size = gram.shape[0]
    b = 64
    w[:, :size] = gram[...]
    ids = lax.broadcasted_iota(jnp.int32, (size, size), 0)
    lanes = lax.broadcasted_iota(jnp.int32, (size, size), 1)
    w[:, size:] = jnp.where(ids == lanes, 1.0, 0.0).astype(F32)
    for o in range(0, size, b):
        base = o // 128 * 128
        side = o - base
        x = eliminate(w[o:o + b, base:base + 128], side)
        block = w[o:o + b, :]
        zero = jnp.zeros_like(block)
        stack = jnp.concatenate([zero, block] if side == 0 else [block, zero], axis=0)
        strip = dot(x, stack, 1, 0)
        w[o:o + b, :] = strip
        if o + b < size:
            update = dot(strip[:, :size], strip, 0, 0)
            w[o + b:, :] = w[o + b:, :] - update[o + b:, :]
    result = dot(proj[...], w[:, size:], 1, 1)
    ortho[...] = result
    left[...] = result * scale


def back_kernel(
    R, F, T, mom, grad, bmean, ortho, right_out, mom_out,
    bp, zrecv, full, sq, sqrecv,
    z_send, z_recv, a_send, a_recv, r_send, r_recv, s_send, s_recv,
):
    at = Place(R, F, T)
    cols = mom.shape[2]
    piece = bp.shape[1]
    rank = ortho.shape[1]
    tens = [{"tensor": lax.rem(at.t + d, T)} for d in range(1, T)]
    back = dot(bmean[...], ortho[...], 0, 0)
    for g in range(F):
        bp[g] = back[g * piece:(g + 1) * piece, :]
    greet([at.rep(d)[1] for d in range(1, R)] + [at.line(d)[1] for d in range(1, F)] + tens)

    sent = []
    for d in range(1, F):
        q, where = at.line(d)
        copy = remote(bp.at[q], zrecv.at[at.f], z_send.at[d - 1], z_recv.at[at.f], where)
        copy.start()
        sent.append(copy)
    zrecv[at.f] = bp[at.f]
    for d in range(1, F):
        q = at.line_from(d)
        remote(bp.at[q], zrecv.at[q], z_send.at[d - 1], z_recv.at[q], at.line(d)[1]).wait_recv()
    total = zrecv[0]
    for k in range(1, F):
        total = total + zrecv[k]
    full[at.r, at.f] = total

    def forward(f, i):
        for d in range(1, R):
            q, where = at.rep(d)
            copy = remote(full.at[at.r, f], full.at[at.r, f], r_send.at[i, d - 1], r_recv.at[at.r, f], where)
            copy.start()
            sent.append(copy)

    forward(at.f, 0)
    for d in range(1, F):
        q, where = at.line(d)
        copy = remote(full.at[at.r, at.f], full.at[at.r, at.f], a_send.at[d - 1], a_recv.at[at.f], where)
        copy.start()
        sent.append(copy)
    for d in range(1, F):
        q = at.line_from(d)
        remote(full.at[at.r, q], full.at[at.r, q], a_send.at[d - 1], a_recv.at[q], at.line(d)[1]).wait_recv()
        forward(q, d)
    for i in range(F):
        g = at.line_from(i)
        for d in range(1, R):
            k = at.rep_from(d)
            remote(full.at[k, g], full.at[k, g], r_send.at[i, d - 1], r_recv.at[k, g], at.rep(d)[1]).wait_recv()

    squares = jnp.zeros((1, rank), F32)
    for k in range(R):
        for g in range(F):
            v = full[k, g]
            squares = squares + jnp.sum(v * v, axis=0, keepdims=True)
    sq[...] = jnp.broadcast_to(squares, sq.shape)
    for d in range(1, T):
        copy = remote(sq, sqrecv.at[at.t], s_send.at[d - 1], s_recv.at[at.t], tens[d - 1])
        copy.start()
        sent.append(copy)
    sqrecv[at.t] = sq[...]

    o = ortho[...] * -0.1
    for k in range(R):
        if (k + 1) % 2:
            continue
        block = jnp.concatenate([full[j, g] for j in (k - 1, k) for g in range(F)], axis=0)
        span = block.shape[0]
        first = (k - 1) // 2 * span
        here = slice(first, first + span)
        mom_out[0, :, here] = mom[0, :, here] + grad[0, :, here].astype(F32) + dot(o, block, 1, 1)

    for d in range(1, T):
        k = lax.rem(at.t + T - d, T)
        remote(sq, sqrecv.at[k], s_send.at[d - 1], s_recv.at[k], tens[d - 1]).wait_recv()
    total = sqrecv[0]
    for k in range(1, T):
        total = total + sqrecv[k]
    norm = jnp.sqrt(total[0:1, :] + 1e-06)
    scale = math.sqrt(cols * T) / norm
    for i in range(R):
        k = at.f * R + i
        right_out[i * piece:(i + 1) * piece, :] = full[k // F, lax.rem(k, F)] * scale
    for copy in sent:
        copy.wait_send()


def solution(mesh):
    R, F, T = mesh.shape["replica"], mesh.shape["fsdp"], mesh.shape["tensor"]
    n = R * T
    DMA = pltpu.SemaphoreType.DMA

    def shards(momentum, gradient, right_in):
        rows, cols = momentum.shape[1], momentum.shape[2]
        qb, rank = right_in.shape
        share = cols // R
        nb = F // R
        nc = 4 if qb % 32 == 0 else 1
        piece = share // F
        sds = jax.ShapeDtypeStruct
        slots = lambda m, r: pltpu.VMEM((m, r, rank), F32)
        bmean, proj, gram = pl.pallas_call(
            lambda *refs: project_kernel(R, F, T, *refs),
            out_shape=(sds((rows, share), F32), sds((rows, rank), F32), sds((rank, rank), F32)),
            in_specs=vmem(3),
            out_specs=tuple(vmem(3)),
            scratch_shapes=[
                pltpu.VMEM((R, rows, share), F32),
                pltpu.VMEM((R, rows, share), F32),
                pltpu.VMEM((nb, nc, qb // nc, rank), F32),
                slots(n, rows // n),
                slots(n, rows // n),
                slots(n, rows // n),
                slots(n, rank // n),
                slots(F, rank // n),
                slots(n, rank // n),
                DMA((R,)), DMA((R,)),
                DMA((nb, nc)), DMA((nb, nc)), DMA((nb, nc)),
                DMA((n,)), DMA((n,)), DMA((n,)), DMA((n,)),
                DMA((F,)), DMA((F,)), DMA((n,)), DMA((n,)),
            ],
            compiler_params=pltpu.CompilerParams(
                collective_id=0, has_side_effects=True, vmem_limit_bytes=40 << 20
            ),
            name="project",
        )(momentum, gradient, right_in)
        ortho, left = pl.pallas_call(
            lambda *refs: factor_kernel(math.sqrt(rows * F), *refs),
            out_shape=(sds((rows, rank), F32), sds((rows, rank), F32)),
            in_specs=vmem(2),
            out_specs=tuple(vmem(2)),
            scratch_shapes=[pltpu.VMEM((rank, 2 * rank), F32)],
            compiler_params=pltpu.CompilerParams(vmem_limit_bytes=40 << 20),
            name="factor",
        )(gram, proj)
        right, updated = pl.pallas_call(
            lambda *refs: back_kernel(R, F, T, *refs),
            out_shape=(sds((qb, rank), F32), sds(momentum.shape, F32)),
            in_specs=vmem(4),
            out_specs=tuple(vmem(2)),
            scratch_shapes=[
                slots(F, piece),
                slots(F, piece),
                pltpu.VMEM((R, F, piece, rank), F32),
                pltpu.VMEM((8, rank), F32),
                slots(T, 8),
                DMA((F,)), DMA((F,)), DMA((F,)), DMA((F,)),
                DMA((F, R)), DMA((R, F)), DMA((T,)), DMA((T,)),
            ],
            compiler_params=pltpu.CompilerParams(
                collective_id=1, has_side_effects=True, vmem_limit_bytes=40 << 20
            ),
            name="back",
        )(momentum, gradient, bmean, ortho)
        return left, right, updated

    placed = (
        P("replica", "fsdp", "tensor"),
        P("replica", "fsdp", "tensor"),
        P(("tensor", "fsdp"), None),
    )
    return jax.shard_map(
        shards,
        mesh=mesh,
        in_specs=placed,
        out_specs=(P("fsdp", None), P(("tensor", "fsdp"), None), P("replica", "fsdp", "tensor")),
        check_vma=False,
    )
```

```python
import math

import jax
import jax.numpy as jnp
from jax import lax
from jax.experimental import pallas as pl
from jax.experimental.pallas import tpu as pltpu
from jax.sharding import PartitionSpec as P

MESH = pl.DeviceIdType.MESH
HIGHEST = lax.Precision.HIGHEST
F32 = jnp.float32


def dot(a, b, ca, cb):
    return lax.dot_general(
        a, b, (((ca,), (cb,)), ((), ())), precision=HIGHEST, preferred_element_type=F32
    )


def vmem(n):
    return [pl.BlockSpec(memory_space=pltpu.VMEM)] * n


def hbm(n):
    return [pl.BlockSpec(memory_space=pl.ANY)] * n


class Place:
    def __init__(self, R, F, T):
        self.R, self.F, self.T, self.n = R, F, T, R * T
        self.r = lax.axis_index("replica")
        self.f = lax.axis_index("fsdp")
        self.t = lax.axis_index("tensor")
        self.p = self.r * T + self.t

    def plane(self, d):
        q = lax.rem(self.p + d, self.n)
        return q, {"replica": q // self.T, "tensor": lax.rem(q, self.T)}

    def plane_from(self, d):
        return lax.rem(self.p + self.n - d, self.n)

    def line(self, d):
        q = lax.rem(self.f + d, self.F)
        return q, {"fsdp": q}

    def line_from(self, d):
        return lax.rem(self.f + self.F - d, self.F)

    def cross(self):
        low = lax.rem(self.r, 2)
        return self.r + 1 - 2 * low, lax.rem(self.r + 2, 4), 3 - self.r

    def rep(self, d):
        q = lax.rem(self.r + d, self.R)
        return q, {"replica": q}

    def rep_from(self, d):
        return lax.rem(self.r + self.R - d, self.R)


def remote(src, dst, send, recv, where):
    return pltpu.make_async_remote_copy(
        src_ref=src, dst_ref=dst, send_sem=send, recv_sem=recv, device_id=where, device_id_type=MESH
    )


def greet(targets):
    barrier = pltpu.get_barrier_semaphore()
    for where in targets:
        pl.semaphore_signal(barrier, inc=1, device_id=where, device_id_type=MESH)
    pl.semaphore_wait(barrier, len(targets))


def pack(part):
    rows, share = part.shape
    whole = share // 128 * 128
    tiles = [part[:, i:i + 128] for i in range(0, whole, 128)]
    if whole < share:
        half = rows // 2
        tiles.append(jnp.concatenate([part[:half, whole:], part[half:, whole:]], axis=1))
    return jnp.concatenate(tiles, axis=0)


def unpack(flat, rows, share):
    whole = share // 128 * 128
    tiles = [flat[i * rows:(i + 1) * rows] for i in range(whole // 128)]
    if whole < share:
        last = flat[whole // 128 * rows:]
        tiles.append(jnp.concatenate([last[:, :64], last[:, 64:]], axis=0))
    return jnp.concatenate(tiles, axis=1)


def project_kernel(
    R, F, T, mom_in, grad_in, q_in, bmean_out, proj_out, gram_out,
    mom, grad, bufs, brecv, qs, pp, precv, proj, gp, grecv, gram,
    in_sem, q_sem, b_send, b_recv, q_up, q_down, q_recv, p_send, p_recv, a_send, a_recv,
    g_send, g_recv, h_send, h_recv,
):
    at = Place(R, F, T)
    rows, cols = mom.shape
    share = cols // R
    n = at.n
    loads = [
        pltpu.make_async_copy(mom_in.at[0], mom, in_sem.at[0]),
        pltpu.make_async_copy(grad_in.at[0], grad, in_sem.at[1]),
    ]
    for copy in loads:
        copy.start()
    nb = F // R
    nc, qc = qs.shape[1], qs.shape[2]

    def fetch(j, c):
        return pltpu.make_async_copy(q_in.at[pl.ds(c * qc, qc)], qs.at[j, c], q_sem.at[j, c])

    for j in range(nb):
        @pl.when(at.f == at.r * nb + j)
        def _():
            for c in range(nc):
                fetch(j, c).start()

    greet([at.plane(d)[1] for d in range(1, n)] + [at.line(d)[1] for d in range(1, F)])

    for copy in loads:
        copy.wait()
    half = bufs.shape[2]
    for k in range(R):
        part = slice(k * share, (k + 1) * share)
        flat = pack(mom[:, part] + grad[:, part].astype(F32))
        for h in range(2):
            bufs[k, h] = flat[h * half:(h + 1) * half]

    rx, ry, rd = at.cross()
    sent = []

    def hop(src, h, slot, k):
        return remote(bufs.at[src, h], brecv.at[h, slot], b_send.at[h, slot], b_recv.at[h, slot], {"replica": k})

    for slot in range(2):
        for h, first in enumerate((rx, ry)):
            copy = hop((rd, first)[slot], h, slot, first)
            copy.start()
            sent.append(copy)

    def up(j, c):
        return remote(qs.at[j, c], qs.at[j, c], q_up.at[j, c], q_recv.at[j, c], {"fsdp": lax.rem(at.f + 1, F)})

    def down(j, c):
        return remote(qs.at[j, c], qs.at[j, c], q_down.at[j, c], q_recv.at[j, c], {"fsdp": lax.rem(at.f + F - 1, F)})

    def pass_on(c, j):
        home = at.r * nb + j
        @pl.when(at.f == home)
        def _():
            fetch(j, c).wait()
        @pl.when(at.f != home)
        def _():
            up(j, c).wait_recv()
        @pl.when((at.f >= home) & (at.f < F - 1))
        def _():
            up(j, c).start()
        @pl.when((at.f <= home) & (at.f > 0))
        def _():
            down(j, c).start()

    for c in range(nc):
        for j in range(nb):
            pass_on(c, j)
        if c == 0:
            for h, second in enumerate((ry, rx)):
                hop(rd, h, 0, second).wait_recv()
                bufs[second, h] = bufs[second, h] + brecv[h, 0]
                copy = hop(second, h, 2, second)
                copy.start()
                sent.append(copy)
    for h, (first, second) in enumerate(((rx, ry), (ry, rx))):
        hop(first, h, 1, first).wait_recv()
    for h, second in enumerate((ry, rx)):
        hop(second, h, 2, second).wait_recv()
    flat = jnp.concatenate([bufs[at.r, h] + brecv[h, 1] + brecv[h, 2] for h in range(2)], axis=0)
    bmean = unpack(flat * (1.0 / R), rows, share)
    bmean_out[...] = bmean
    part = dot(bmean, qs[...].reshape(share, q_in.shape[1]), 1, 0)
    pp[...] = part.reshape(pp.shape)

    for d in range(1, n):
        q, where = at.plane(d)
        copy = remote(pp.at[q], precv.at[at.p], p_send.at[d - 1], p_recv.at[at.p], where)
        copy.start()
        sent.append(copy)
    precv[at.p] = pp[at.p]
    for d in range(1, n):
        q = at.plane_from(d)
        remote(pp.at[q], precv.at[q], p_send.at[d - 1], p_recv.at[q], at.plane(d)[1]).wait_recv()
    total = precv[0]
    for k in range(1, n):
        total = total + precv[k]
    proj[at.p] = total
    for d in range(1, n):
        q, where = at.plane(d)
        copy = remote(proj.at[at.p], proj.at[at.p], a_send.at[d - 1], a_recv.at[at.p], where)
        copy.start()
        sent.append(copy)
    for d in range(1, n):
        q = at.plane_from(d)
        remote(proj.at[q], proj.at[q], a_send.at[d - 1], a_recv.at[q], at.plane(d)[1]).wait_recv()
    whole = proj[...].reshape(rows, q_in.shape[1])
    proj_out[...] = whole

    gp[...] = dot(whole, whole, 0, 0).reshape(gp.shape)
    for d in range(1, F):
        q, where = at.line(d)
        copy = remote(gp.at[at.p], grecv.at[at.f], g_send.at[d - 1], g_recv.at[at.f], where)
        copy.start()
        sent.append(copy)
    grecv[at.f] = gp[at.p]
    for d in range(1, F):
        q = at.line_from(d)
        remote(gp.at[at.p], grecv.at[q], g_send.at[d - 1], g_recv.at[q], at.line(d)[1]).wait_recv()
    total = grecv[0]
    for k in range(1, F):
        total = total + grecv[k]
    gram[at.p] = total
    for d in range(1, n):
        q, where = at.plane(d)
        copy = remote(gram.at[at.p], gram.at[at.p], h_send.at[d - 1], h_recv.at[at.p], where)
        copy.start()
        sent.append(copy)
    for d in range(1, n):
        q = at.plane_from(d)
        remote(gram.at[q], gram.at[q], h_send.at[d - 1], h_recv.at[q], at.plane(d)[1]).wait_recv()
    gram_out[...] = gram[...].reshape(gram_out.shape)

    for copy in sent:
        copy.wait_send()
    for c in range(nc):
        for j in range(nb):
            home = at.r * nb + j
            @pl.when((at.f >= home) & (at.f < F - 1))
            def _():
                up(j, c).wait_send()
            @pl.when((at.f <= home) & (at.f > 0))
            def _():
                down(j, c).wait_send()


def eliminate(tile, side):
    b = tile.shape[0]
    rows_id = lax.broadcasted_iota(jnp.int32, tile.shape, 0)
    lanes = lax.broadcasted_iota(jnp.int32, tile.shape, 1)
    other = b - side
    inside = (lanes >= side) & (lanes < side + b)
    x = jnp.where(inside, tile, jnp.where(lanes - other == rows_id, 1.0, 0.0).astype(F32))
    done = []
    for k0 in range(0, b, 8):
        shape = x.shape
        ids = lax.broadcasted_iota(jnp.int32, shape, 0)
        panel = [
            jnp.broadcast_to(x[:, side + k0 + j:side + k0 + j + 1], shape) for j in range(8)
        ]
        for j in range(8):
            inverse = 1.0 / panel[j][j:j + 1, :]
            scale = jnp.where(ids > j, panel[j], 0.0) * inverse
            for i in range(j + 1, 8):
                panel[i] = panel[i] - scale * panel[i][j:j + 1, :]
            x = x - scale * x[j:j + 1, :]
        done.append(x[:8])
        x = x[8:]
    x = jnp.concatenate(done, axis=0)
    pivot = jnp.sum(jnp.where(lanes - side == rows_id, x, 0.0), axis=1, keepdims=True)
    return x * (1.0 / jnp.sqrt(pivot))


def factor_kernel(scale, gram, proj, ortho, left, w):
    size = gram.shape[0]
    b = 64
    w[:, :size] = gram[...]
    ids = lax.broadcasted_iota(jnp.int32, (size, size), 0)
    lanes = lax.broadcasted_iota(jnp.int32, (size, size), 1)
    w[:, size:] = jnp.where(ids == lanes, 1.0, 0.0).astype(F32)
    for o in range(0, size, b):
        base = o // 128 * 128
        side = o - base
        x = eliminate(w[o:o + b, base:base + 128], side)
        block = w[o:o + b, :]
        zero = jnp.zeros_like(block)
        stack = jnp.concatenate([zero, block] if side == 0 else [block, zero], axis=0)
        strip = dot(x, stack, 1, 0)
        w[o:o + b, :] = strip
        if o + b < size:
            update = dot(strip[:, :size], strip, 0, 0)
            w[o + b:, :] = w[o + b:, :] - update[o + b:, :]
    result = dot(proj[...], w[:, size:], 1, 1)
    ortho[...] = result
    left[...] = result * scale


def back_kernel(
    R, F, T, mom_in, grad_in, bmean, ortho, right_out, mom_out,
    mom, grad, bp, zrecv, full, sq, sqrecv,
    in_sem, out_sem, z_send, z_recv, a_send, a_recv, r_send, r_recv, x_send, s_send, s_recv,
):
    at = Place(R, F, T)
    loads = [
        pltpu.make_async_copy(mom_in.at[0], mom, in_sem.at[0]),
        pltpu.make_async_copy(grad_in.at[0], grad, in_sem.at[1]),
    ]
    for copy in loads:
        copy.start()
    cols = mom.shape[1]
    parts, sub = bp.shape[1], bp.shape[2]
    piece = parts * sub
    rank = ortho.shape[1]
    tens = [{"tensor": lax.rem(at.t + d, T)} for d in range(1, T)]
    rx, ry, rd = at.cross()
    back = dot(bmean[...], ortho[...], 0, 0)
    for g in range(F):
        for h in range(parts):
            bp[g, h] = back[g * piece + h * sub:g * piece + (h + 1) * sub, :]
    greet([{"replica": rx}, {"replica": ry}] + [at.line(d)[1] for d in range(1, F)] + tens)

    sent = []

    def go(copy):
        copy.start()
        sent.append(copy)

    for h in range(parts):
        for d in range(1, F):
            q, where = at.line(d)
            go(remote(bp.at[q, h], zrecv.at[at.f, h], z_send.at[h, d], z_recv.at[h, at.f], where))

    def share_out(h, i):
        g = at.line_from(i)
        slot = full.at[at.r, g, h]
        for e, k in enumerate((rx, ry)):
            go(remote(slot, slot, r_send.at[h, i, e], r_recv.at[at.r, g, h], {"replica": k}))

    def arrive(k, g, h):
        slot = full.at[k, g, h]
        remote(slot, slot, r_send.at[h, 0, 0], r_recv.at[k, g, h], {"replica": rx}).wait_recv()

    def cross_on(h, i):
        g = at.line_from(i)
        odd = lax.rem(g, 2)
        arrive(rx, g, h)
        arrive(ry, g, h)
        src = rx + (ry - rx) * odd
        dst = ry + (rx - ry) * odd
        slot = full.at[src, g, h]
        go(remote(slot, slot, x_send.at[h, i], r_recv.at[src, g, h], {"replica": dst}))

    for h in range(parts):
        zrecv[at.f, h] = bp[at.f, h]
        for d in range(1, F):
            q = at.line_from(d)
            remote(bp.at[q, h], zrecv.at[q, h], z_send.at[h, d], z_recv.at[h, q], at.line(d)[1]).wait_recv()
        total = zrecv[0, h]
        for k in range(1, F):
            total = total + zrecv[k, h]
        full[at.r, at.f, h] = total
        slot = full.at[at.r, at.f, h]
        for d in range(1, F):
            q, where = at.line(d)
            go(remote(slot, slot, a_send.at[h, d], a_recv.at[h, at.f], where))
        share_out(h, 0)
    order = [(h, i) for h in range(parts) for i in range(1, F)]
    late = [(h, 0) for h in range(parts)]
    for h, i in order:
        q = at.line_from(i)
        slot = full.at[at.r, q, h]
        remote(slot, slot, a_send.at[h, i], a_recv.at[h, q], at.line(i)[1]).wait_recv()
        share_out(h, i)
        late.append((h, i))
        cross_on(*late.pop(0))
    for h, i in late:
        cross_on(h, i)
    for h in range(parts):
        for i in range(F):
            arrive(rd, at.line_from(i), h)

    squares = jnp.zeros((1, rank), F32)
    for k in range(R):
        for g in range(F):
            for h in range(parts):
                v = full[k, g, h]
                squares = squares + jnp.sum(v * v, axis=0, keepdims=True)
    sq[...] = jnp.broadcast_to(squares, sq.shape)
    for d in range(1, T):
        go(remote(sq, sqrecv.at[at.t], s_send.at[d], s_recv.at[at.t], tens[d - 1]))
    sqrecv[at.t] = sq[...]

    for copy in loads:
        copy.wait()
    o = ortho[...] * -0.1
    stores = []
    for m in range(2):
        block = jnp.concatenate(
            [full[k, g, h] for k in range(m * R // 2, (m + 1) * R // 2) for g in range(F) for h in range(parts)], axis=0
        )
        here = pl.ds(m * (cols // 2), cols // 2)
        mom[:, here] = mom[:, here] + grad[:, here].astype(F32) + dot(o, block, 1, 1)
        copy = pltpu.make_async_copy(mom.at[:, here], mom_out.at[0, :, here], out_sem.at[m])
        copy.start()
        stores.append(copy)

    for d in range(1, T):
        k = lax.rem(at.t + T - d, T)
        remote(sq, sqrecv.at[k], s_send.at[d], s_recv.at[k], tens[d - 1]).wait_recv()
    total = sqrecv[0]
    for k in range(1, T):
        total = total + sqrecv[k]
    norm = jnp.sqrt(total[0:1, :] + 1e-06)
    scale = math.sqrt(cols * T) / norm
    for i in range(R):
        k = at.f * R + i
        for h in range(parts):
            first = i * piece + h * sub
            right_out[first:first + sub, :] = full[k // F, lax.rem(k, F), h] * scale
    for copy in stores:
        copy.wait()
    for copy in sent:
        copy.wait_send()


def solution(mesh):
    R, F, T = mesh.shape["replica"], mesh.shape["fsdp"], mesh.shape["tensor"]
    n = R * T
    DMA = pltpu.SemaphoreType.DMA

    def shards(momentum, gradient, right_in):
        rows, cols = momentum.shape[1], momentum.shape[2]
        qb, rank = right_in.shape
        share = cols // R
        nb = F // R
        nc = 4 if qb % 32 == 0 else 1
        piece = share // F
        parts = 2
        sds = jax.ShapeDtypeStruct
        slots = lambda m, r: pltpu.VMEM((m, r, rank), F32)
        bmean, proj, gram = pl.pallas_call(
            lambda *refs: project_kernel(R, F, T, *refs),
            out_shape=(sds((rows, share), F32), sds((rows, rank), F32), sds((rank, rank), F32)),
            in_specs=hbm(3),
            out_specs=tuple(vmem(3)),
            scratch_shapes=[
                pltpu.VMEM((rows, cols), F32),
                pltpu.VMEM((rows, cols), gradient.dtype),
                pltpu.VMEM((R, 2, rows * share // 256, 128), F32),
                pltpu.VMEM((2, 3, rows * share // 256, 128), F32),
                pltpu.VMEM((nb, nc, qb // nc, rank), F32),
                slots(n, rows // n),
                slots(n, rows // n),
                slots(n, rows // n),
                slots(n, rank // n),
                slots(F, rank // n),
                slots(n, rank // n),
                DMA((2,)), DMA((nb, nc)), DMA((2, 3)), DMA((2, 3)),
                DMA((nb, nc)), DMA((nb, nc)), DMA((nb, nc)),
                DMA((n,)), DMA((n,)), DMA((n,)), DMA((n,)),
                DMA((F,)), DMA((F,)), DMA((n,)), DMA((n,)),
            ],
            compiler_params=pltpu.CompilerParams(
                collective_id=0, has_side_effects=True, vmem_limit_bytes=40 << 20
            ),
            name="project",
        )(momentum, gradient, right_in)
        ortho, left = pl.pallas_call(
            lambda *refs: factor_kernel(math.sqrt(rows * F), *refs),
            out_shape=(sds((rows, rank), F32), sds((rows, rank), F32)),
            in_specs=vmem(2),
            out_specs=tuple(vmem(2)),
            scratch_shapes=[pltpu.VMEM((rank, 2 * rank), F32)],
            compiler_params=pltpu.CompilerParams(vmem_limit_bytes=40 << 20),
            name="factor",
        )(gram, proj)
        right, updated = pl.pallas_call(
            lambda *refs: back_kernel(R, F, T, *refs),
            out_shape=(sds((qb, rank), F32), sds(momentum.shape, F32)),
            in_specs=hbm(2) + vmem(2),
            out_specs=(vmem(1) + hbm(1)),
            scratch_shapes=[
                pltpu.VMEM((rows, cols), F32),
                pltpu.VMEM((rows, cols), gradient.dtype),
                pltpu.VMEM((F, parts, piece // parts, rank), F32),
                pltpu.VMEM((F, parts, piece // parts, rank), F32),
                pltpu.VMEM((R, F, parts, piece // parts, rank), F32),
                pltpu.VMEM((8, rank), F32),
                slots(T, 8),
                DMA((2,)), DMA((2,)),
                DMA((parts, F)), DMA((parts, F)), DMA((parts, F)), DMA((parts, F)),
                DMA((parts, F, 2)), DMA((R, F, parts)), DMA((parts, F)), DMA((T,)), DMA((T,)),
            ],
            compiler_params=pltpu.CompilerParams(
                collective_id=1, has_side_effects=True, vmem_limit_bytes=40 << 20
            ),
            name="back",
        )(momentum, gradient, bmean, ortho)
        return left, right, updated

    placed = (
        P("replica", "fsdp", "tensor"),
        P("replica", "fsdp", "tensor"),
        P(("tensor", "fsdp"), None),
    )
    return jax.shard_map(
        shards,
        mesh=mesh,
        in_specs=placed,
        out_specs=(P("fsdp", None), P(("tensor", "fsdp"), None), P("replica", "fsdp", "tensor")),
        check_vma=False,
    )
```

```python
import math

import jax
import jax.numpy as jnp
from jax import lax
from jax.experimental import pallas as pl
from jax.experimental.pallas import tpu as pltpu
from jax.sharding import PartitionSpec as P

MESH = pl.DeviceIdType.MESH
HIGHEST = lax.Precision.HIGHEST
F32 = jnp.float32


def dot(a, b, ca, cb):
    return lax.dot_general(
        a, b, (((ca,), (cb,)), ((), ())), precision=HIGHEST, preferred_element_type=F32
    )


def halves(a):
    high = a.astype(jnp.bfloat16)
    return high, (a - high.astype(F32)).astype(jnp.bfloat16)


def dot3(a, b, ca, cb):
    ah, al = halves(a)
    bh, bl = halves(b)
    one = lambda x, y: lax.dot_general(x, y, (((ca,), (cb,)), ((), ())), preferred_element_type=F32)
    return one(ah, bh) + (one(ah, bl) + one(al, bh))


def vmem(n):
    return [pl.BlockSpec(memory_space=pltpu.VMEM)] * n


def hbm(n):
    return [pl.BlockSpec(memory_space=pltpu.HBM)] * n


class Place:
    def __init__(self, R, F, T):
        self.R, self.F, self.T, self.n = R, F, T, R * T
        self.r = lax.axis_index("replica")
        self.f = lax.axis_index("fsdp")
        self.t = lax.axis_index("tensor")
        self.p = self.r * T + self.t

    def plane(self, d):
        q = lax.rem(self.p + d, self.n)
        return q, {"replica": q // self.T, "tensor": lax.rem(q, self.T)}

    def plane_from(self, d):
        return lax.rem(self.p + self.n - d, self.n)

    def line(self, d):
        q = lax.rem(self.f + d, self.F)
        return q, {"fsdp": q}

    def line_from(self, d):
        return lax.rem(self.f + self.F - d, self.F)

    def cross(self):
        low = lax.rem(self.r, 2)
        return self.r + 1 - 2 * low, lax.rem(self.r + 2, 4), 3 - self.r

    def rep(self, d):
        q = lax.rem(self.r + d, self.R)
        return q, {"replica": q}

    def rep_from(self, d):
        return lax.rem(self.r + self.R - d, self.R)


def remote(src, dst, send, recv, where):
    return pltpu.make_async_remote_copy(
        src_ref=src, dst_ref=dst, send_sem=send, recv_sem=recv, device_id=where, device_id_type=MESH
    )


def greet(targets):
    barrier = pltpu.get_barrier_semaphore()
    for where in targets:
        pl.semaphore_signal(barrier, inc=1, device_id=where, device_id_type=MESH)
    pl.semaphore_wait(barrier, len(targets))


def pack(part):
    rows, share = part.shape
    whole = share // 128 * 128
    tiles = [part[:, i:i + 128] for i in range(0, whole, 128)]
    if whole < share:
        half = rows // 2
        tiles.append(jnp.concatenate([part[:half, whole:], part[half:, whole:]], axis=1))
    return jnp.concatenate(tiles, axis=0)


def unpack(flat, rows, share):
    whole = share // 128 * 128
    tiles = [flat[i * rows:(i + 1) * rows] for i in range(whole // 128)]
    if whole < share:
        last = flat[whole // 128 * rows:]
        tiles.append(jnp.concatenate([last[:, :64], last[:, 64:]], axis=0))
    return jnp.concatenate(tiles, axis=1)


def project_kernel(
    R, F, T, mom_in, grad_in, q_in, bmean_out, proj_out, gram_out,
    mom, grad, bufs, brecv, qs, pp, precv, proj, gp, grecv, gram,
    in_sem, q_sem, b_send, b_recv, q_up, q_down, q_recv, p_send, p_recv, a_send, a_recv,
    g_send, g_recv, h_send, h_recv,
):
    at = Place(R, F, T)
    rows, cols = mom.shape
    share = cols // R
    n = at.n
    loads = [
        pltpu.make_async_copy(mom_in.at[0], mom, in_sem.at[0]),
        pltpu.make_async_copy(grad_in.at[0], grad, in_sem.at[1]),
    ]
    for copy in loads:
        copy.start()
    nb = F // R
    nc, qc = qs.shape[1], qs.shape[2]

    def fetch(j, c):
        return pltpu.make_async_copy(q_in.at[pl.ds(c * qc, qc)], qs.at[j, c], q_sem.at[j, c])

    for j in range(nb):
        @pl.when(at.f == at.r * nb + j)
        def _():
            for c in range(nc):
                fetch(j, c).start()

    greet([at.plane(d)[1] for d in range(1, n)] + [at.line(d)[1] for d in range(1, F)])

    for copy in loads:
        copy.wait()
    half = bufs.shape[2]
    for k in range(R):
        part = slice(k * share, (k + 1) * share)
        flat = pack(mom[:, part] + grad[:, part].astype(F32))
        for h in range(2):
            bufs[k, h] = flat[h * half:(h + 1) * half]

    rx, ry, rd = at.cross()
    sent = []

    def hop(src, h, slot, k):
        return remote(bufs.at[src, h], brecv.at[h, slot], b_send.at[h, slot], b_recv.at[h, slot], {"replica": k})

    for slot in range(2):
        for h, first in enumerate((rx, ry)):
            copy = hop((rd, first)[slot], h, slot, first)
            copy.start()
            sent.append(copy)

    def up(j, c):
        return remote(qs.at[j, c], qs.at[j, c], q_up.at[j, c], q_recv.at[j, c], {"fsdp": lax.rem(at.f + 1, F)})

    def down(j, c):
        return remote(qs.at[j, c], qs.at[j, c], q_down.at[j, c], q_recv.at[j, c], {"fsdp": lax.rem(at.f + F - 1, F)})

    def pass_on(c, j):
        home = at.r * nb + j
        @pl.when(at.f == home)
        def _():
            fetch(j, c).wait()
        @pl.when(at.f != home)
        def _():
            up(j, c).wait_recv()
        @pl.when((at.f >= home) & (at.f < F - 1))
        def _():
            up(j, c).start()
        @pl.when((at.f <= home) & (at.f > 0))
        def _():
            down(j, c).start()

    for c in range(nc):
        for j in range(nb):
            pass_on(c, j)
        if c == 0:
            for h, second in enumerate((ry, rx)):
                hop(rd, h, 0, second).wait_recv()
                bufs[second, h] = bufs[second, h] + brecv[h, 0]
                copy = hop(second, h, 2, second)
                copy.start()
                sent.append(copy)
    for h, (first, second) in enumerate(((rx, ry), (ry, rx))):
        hop(first, h, 1, first).wait_recv()
    for h, second in enumerate((ry, rx)):
        hop(second, h, 2, second).wait_recv()
    flat = jnp.concatenate([bufs[at.r, h] + brecv[h, 1] + brecv[h, 2] for h in range(2)], axis=0)
    bmean = unpack(flat * (1.0 / R), rows, share)
    bmean_out[...] = bmean
    part = dot(bmean, qs[...].reshape(share, q_in.shape[1]), 1, 0)
    pp[...] = part.reshape(pp.shape)

    for d in range(1, n):
        q, where = at.plane(d)
        copy = remote(pp.at[q], precv.at[at.p], p_send.at[d - 1], p_recv.at[at.p], where)
        copy.start()
        sent.append(copy)
    precv[at.p] = pp[at.p]
    for d in range(1, n):
        q = at.plane_from(d)
        remote(pp.at[q], precv.at[q], p_send.at[d - 1], p_recv.at[q], at.plane(d)[1]).wait_recv()
    total = precv[0]
    for k in range(1, n):
        total = total + precv[k]
    proj[at.p] = total
    for d in range(1, n):
        q, where = at.plane(d)
        copy = remote(proj.at[at.p], proj.at[at.p], a_send.at[d - 1], a_recv.at[at.p], where)
        copy.start()
        sent.append(copy)
    for d in range(1, n):
        q = at.plane_from(d)
        remote(proj.at[q], proj.at[q], a_send.at[d - 1], a_recv.at[q], at.plane(d)[1]).wait_recv()
    whole = proj[...].reshape(rows, q_in.shape[1])
    proj_out[...] = whole

    gp[...] = dot(whole, whole, 0, 0).reshape(gp.shape)
    for d in range(1, F):
        q, where = at.line(d)
        copy = remote(gp.at[at.p], grecv.at[at.f], g_send.at[d - 1], g_recv.at[at.f], where)
        copy.start()
        sent.append(copy)
    grecv[at.f] = gp[at.p]
    for d in range(1, F):
        q = at.line_from(d)
        remote(gp.at[at.p], grecv.at[q], g_send.at[d - 1], g_recv.at[q], at.line(d)[1]).wait_recv()
    total = grecv[0]
    for k in range(1, F):
        total = total + grecv[k]
    gram[at.p] = total
    for d in range(1, n):
        q, where = at.plane(d)
        copy = remote(gram.at[at.p], gram.at[at.p], h_send.at[d - 1], h_recv.at[at.p], where)
        copy.start()
        sent.append(copy)
    for d in range(1, n):
        q = at.plane_from(d)
        remote(gram.at[q], gram.at[q], h_send.at[d - 1], h_recv.at[q], at.plane(d)[1]).wait_recv()
    gram_out[...] = gram[...].reshape(gram_out.shape)

    for copy in sent:
        copy.wait_send()
    for c in range(nc):
        for j in range(nb):
            home = at.r * nb + j
            @pl.when((at.f >= home) & (at.f < F - 1))
            def _():
                up(j, c).wait_send()
            @pl.when((at.f <= home) & (at.f > 0))
            def _():
                down(j, c).wait_send()


def eliminate(tile, side):
    b = tile.shape[0]
    rows_id = lax.broadcasted_iota(jnp.int32, tile.shape, 0)
    lanes = lax.broadcasted_iota(jnp.int32, tile.shape, 1)
    other = b - side
    inside = (lanes >= side) & (lanes < side + b)
    x = jnp.where(inside, tile, jnp.where(lanes - other == rows_id, 1.0, 0.0).astype(F32))
    done = []
    for k0 in range(0, b, 8):
        shape = x.shape
        ids = lax.broadcasted_iota(jnp.int32, shape, 0)
        panel = [
            jnp.broadcast_to(x[:, side + k0 + j:side + k0 + j + 1], shape) for j in range(8)
        ]
        for j in range(8):
            inverse = 1.0 / panel[j][j:j + 1, :]
            scale = jnp.where(ids > j, panel[j], 0.0) * inverse
            for i in range(j + 1, 8):
                panel[i] = panel[i] - scale * panel[i][j:j + 1, :]
            x = x - scale * x[j:j + 1, :]
        done.append(x[:8])
        x = x[8:]
    x = jnp.concatenate(done, axis=0)
    pivot = jnp.sum(jnp.where(lanes - side == rows_id, x, 0.0), axis=1, keepdims=True)
    return x * (1.0 / jnp.sqrt(pivot))


def factor_kernel(scale, gram, proj, ortho, left, w):
    size = gram.shape[0]
    b = 64
    w[:, :size] = gram[...]
    ids = lax.broadcasted_iota(jnp.int32, (size, size), 0)
    lanes = lax.broadcasted_iota(jnp.int32, (size, size), 1)
    w[:, size:] = jnp.where(ids == lanes, 1.0, 0.0).astype(F32)
    for o in range(0, size, b):
        base = o // 128 * 128
        side = o - base
        x = eliminate(w[o:o + b, base:base + 128], side)
        block = w[o:o + b, :]
        zero = jnp.zeros_like(block)
        stack = jnp.concatenate([zero, block] if side == 0 else [block, zero], axis=0)
        strip = dot(x, stack, 1, 0)
        w[o:o + b, :] = strip
        if o + b < size:
            update = dot(strip[:, :size], strip, 0, 0)
            w[o + b:, :] = w[o + b:, :] - update[o + b:, :]
    result = dot(proj[...], w[:, size:], 1, 1)
    ortho[...] = result
    left[...] = result * scale


def back_kernel(
    R, F, T, mom_in, grad_in, bmean, ortho, right_out, mom_out,
    mom, grad, bp, zrecv, full, sq, sqrecv,
    in_sem, out_sem, z_send, z_recv, a_send, a_recv, r_send, r_recv, x_send, s_send, s_recv,
):
    at = Place(R, F, T)
    loads = [
        pltpu.make_async_copy(mom_in.at[0], mom, in_sem.at[0]),
        pltpu.make_async_copy(grad_in.at[0], grad, in_sem.at[1]),
    ]
    for copy in loads:
        copy.start()
    cols = mom.shape[1]
    parts, sub = bp.shape[1], bp.shape[2]
    piece = parts * sub
    rank = ortho.shape[1]
    tens = [{"tensor": lax.rem(at.t + d, T)} for d in range(1, T)]
    rx, ry, rd = at.cross()
    back = dot(bmean[...], ortho[...], 0, 0)
    for g in range(F):
        for h in range(parts):
            bp[g, h] = back[g * piece + h * sub:g * piece + (h + 1) * sub, :]
    above, below = lax.rem(at.f + 1, F), lax.rem(at.f + F - 1, F)
    sides = ({"fsdp": above}, {"fsdp": below})
    greet([{"replica": rx}, {"replica": ry}] + list(sides) + tens)

    started = []

    def go(make, cond=None):
        started.append((make, cond))
        make().start()

    def partial(e, g, h):
        return remote(bp.at[g, h], zrecv.at[e, g, h], z_send.at[g, h], z_recv.at[e, g, h], sides[e])

    for s in range(F - 1):
        for h in range(parts):
            for e, g in enumerate((F - 1 - s, s)):
                cond = (at.f < g, at.f > g)[e]
                inner = (cond & (at.f > 0), cond & (at.f < F - 1))[e]
                make = lambda e=e, g=g, h=h: partial(e, g, h)
                @pl.when(inner)
                def _():
                    make().wait_recv()
                    bp[g, h] = bp[g, h] + zrecv[e, g, h]
                @pl.when(cond)
                def _():
                    go(make, cond)

    def pass_on(e, g, h):
        slot = full.at[at.r, g, h]
        return remote(slot, slot, a_send.at[e, g, h], a_recv.at[g, h], sides[e])

    def share(e, g, h):
        slot = full.at[at.r, g, h]
        return remote(slot, slot, r_send.at[g, h, e], r_recv.at[at.r, g, h], {"replica": (rx, ry)[e]})

    def arrive(k, g, h):
        slot = full.at[k, g, h]
        remote(slot, slot, r_send.at[g, h, 0], r_recv.at[k, g, h], {"replica": rx}).wait_recv()

    def cross(g, h):
        odd = lax.rem(g, 2)
        src = rx + (ry - rx) * odd
        slot = full.at[src, g, h]
        return remote(slot, slot, x_send.at[g, h], r_recv.at[src, g, h], {"replica": ry + (rx - ry) * odd})

    def cross_on(g, h, cond):
        arrive(rx, g, h)
        arrive(ry, g, h)
        go(lambda: cross(g, h), cond)

    more = (at.f < F - 1, at.f > 0)
    for h in range(parts):
        @pl.when(at.f > 0)
        def _():
            partial(0, at.f, h).wait_recv()
            bp[at.f, h] = bp[at.f, h] + zrecv[0, at.f, h]
        @pl.when(at.f < F - 1)
        def _():
            partial(1, at.f, h).wait_recv()
            bp[at.f, h] = bp[at.f, h] + zrecv[1, at.f, h]
        full[at.r, at.f, h] = bp[at.f, h]
        for e in range(2):
            @pl.when(more[e])
            def _():
                go(lambda e=e, h=h: pass_on(e, at.f, h), more[e])
        for e in range(2):
            go(lambda e=e, h=h: share(e, at.f, h))
    late = [(at.f, h, None) for h in range(parts)]
    for s in range(1, F):
        now = []
        for h in range(parts):
            for e in range(2):
                g = (at.f - s, at.f + s)[e]
                cond = (at.f >= s, at.f < F - s)[e]
                both = cond & more[e]
                @pl.when(cond)
                def _():
                    pass_on(e, g, h).wait_recv()
                @pl.when(both)
                def _():
                    go(lambda e=e, g=g, h=h: pass_on(e, g, h), both)
                @pl.when(cond)
                def _():
                    for i in range(2):
                        go(lambda i=i, g=g, h=h: share(i, g, h), cond)
                now.append((g, h, cond))
        for g, h, cond in late:
            if cond is None:
                cross_on(g, h, None)
            else:
                @pl.when(cond)
                def _():
                    cross_on(g, h, cond)
        late = now
    for g, h, cond in late:
        @pl.when(cond)
        def _():
            cross_on(g, h, cond)
    for g in range(F):
        for h in range(parts):
            arrive(rd, g, h)

    squares = jnp.zeros((1, rank), F32)
    for k in range(R):
        for g in range(F):
            for h in range(parts):
                v = full[k, g, h]
                squares = squares + jnp.sum(v * v, axis=0, keepdims=True)
    sq[...] = jnp.broadcast_to(squares, sq.shape)
    for d in range(1, T):
        go(lambda d=d: remote(sq, sqrecv.at[at.t], s_send.at[d], s_recv.at[at.t], tens[d - 1]))
    sqrecv[at.t] = sq[...]

    for copy in loads:
        copy.wait()
    o = ortho[...] * -0.1
    stores = []
    for m in range(2):
        block = jnp.concatenate(
            [full[k, g, h] for k in range(m * R // 2, (m + 1) * R // 2) for g in range(F) for h in range(parts)], axis=0
        )
        here = pl.ds(m * (cols // 2), cols // 2)
        mom[:, here] = mom[:, here] + grad[:, here].astype(F32) + dot3(o, block, 1, 1)
        copy = pltpu.make_async_copy(mom.at[:, here], mom_out.at[0, :, here], out_sem.at[m])
        copy.start()
        stores.append(copy)

    for d in range(1, T):
        k = lax.rem(at.t + T - d, T)
        remote(sq, sqrecv.at[k], s_send.at[d], s_recv.at[k], tens[d - 1]).wait_recv()
    total = sqrecv[0]
    for k in range(1, T):
        total = total + sqrecv[k]
    norm = jnp.sqrt(total[0:1, :] + 1e-06)
    scale = math.sqrt(cols * T) / norm
    for i in range(R):
        k = at.f * R + i
        for h in range(parts):
            first = i * piece + h * sub
            right_out[first:first + sub, :] = full[k // F, lax.rem(k, F), h] * scale
    for copy in stores:
        copy.wait()
    for make, cond in started:
        if cond is None:
            make().wait_send()
        else:
            @pl.when(cond)
            def _():
                make().wait_send()


def solution(mesh):
    R, F, T = mesh.shape["replica"], mesh.shape["fsdp"], mesh.shape["tensor"]
    n = R * T
    DMA = pltpu.SemaphoreType.DMA

    def shards(momentum, gradient, right_in):
        rows, cols = momentum.shape[1], momentum.shape[2]
        qb, rank = right_in.shape
        share = cols // R
        nb = F // R
        nc = 8 if qb % 64 == 0 else 1
        piece = share // F
        parts = 2
        sds = jax.ShapeDtypeStruct
        slots = lambda m, r: pltpu.VMEM((m, r, rank), F32)
        bmean, proj, gram = pl.pallas_call(
            lambda *refs: project_kernel(R, F, T, *refs),
            out_shape=(sds((rows, share), F32), sds((rows, rank), F32), sds((rank, rank), F32)),
            in_specs=hbm(3),
            out_specs=tuple(vmem(3)),
            scratch_shapes=[
                pltpu.VMEM((rows, cols), F32),
                pltpu.VMEM((rows, cols), gradient.dtype),
                pltpu.VMEM((R, 2, rows * share // 256, 128), F32),
                pltpu.VMEM((2, 3, rows * share // 256, 128), F32),
                pltpu.VMEM((nb, nc, qb // nc, rank), F32),
                slots(n, rows // n),
                slots(n, rows // n),
                slots(n, rows // n),
                slots(n, rank // n),
                slots(F, rank // n),
                slots(n, rank // n),
                DMA((2,)), DMA((nb, nc)), DMA((2, 3)), DMA((2, 3)),
                DMA((nb, nc)), DMA((nb, nc)), DMA((nb, nc)),
                DMA((n,)), DMA((n,)), DMA((n,)), DMA((n,)),
                DMA((F,)), DMA((F,)), DMA((n,)), DMA((n,)),
            ],
            compiler_params=pltpu.CompilerParams(
                collective_id=0, has_side_effects=True, vmem_limit_bytes=60 << 20
            ),
            name="project",
        )(momentum, gradient, right_in)
        ortho, left = pl.pallas_call(
            lambda *refs: factor_kernel(math.sqrt(rows * F), *refs),
            out_shape=(sds((rows, rank), F32), sds((rows, rank), F32)),
            in_specs=vmem(2),
            out_specs=tuple(vmem(2)),
            scratch_shapes=[pltpu.VMEM((rank, 2 * rank), F32)],
            compiler_params=pltpu.CompilerParams(vmem_limit_bytes=60 << 20),
            name="factor",
        )(gram, proj)
        right, updated = pl.pallas_call(
            lambda *refs: back_kernel(R, F, T, *refs),
            out_shape=(sds((qb, rank), F32), sds(momentum.shape, F32)),
            in_specs=hbm(2) + vmem(2),
            out_specs=(vmem(1) + hbm(1)),
            scratch_shapes=[
                pltpu.VMEM((rows, cols), F32),
                pltpu.VMEM((rows, cols), gradient.dtype),
                pltpu.VMEM((F, parts, piece // parts, rank), F32),
                pltpu.VMEM((2, F, parts, piece // parts, rank), F32),
                pltpu.VMEM((R, F, parts, piece // parts, rank), F32),
                pltpu.VMEM((8, rank), F32),
                slots(T, 8),
                DMA((2,)), DMA((2,)),
                DMA((F, parts)), DMA((2, F, parts)), DMA((2, F, parts)), DMA((F, parts)),
                DMA((F, parts, 2)), DMA((R, F, parts)), DMA((F, parts)), DMA((T,)), DMA((T,)),
            ],
            compiler_params=pltpu.CompilerParams(
                collective_id=1, has_side_effects=True, vmem_limit_bytes=60 << 20
            ),
            name="back",
        )(momentum, gradient, bmean, ortho)
        return left, right, updated

    placed = (
        P("replica", "fsdp", "tensor"),
        P("replica", "fsdp", "tensor"),
        P(("tensor", "fsdp"), None),
    )
    return jax.shard_map(
        shards,
        mesh=mesh,
        in_specs=placed,
        out_specs=(P("fsdp", None), P(("tensor", "fsdp"), None), P("replica", "fsdp", "tensor")),
        check_vma=False,
    )
```

```python
import math

import jax
import jax.numpy as jnp
from jax import lax
from jax.experimental import pallas as pl
from jax.experimental.pallas import tpu as pltpu
from jax.sharding import PartitionSpec as P

MESH = pl.DeviceIdType.MESH
HIGHEST = lax.Precision.HIGHEST
F32 = jnp.float32


def dot(a, b, ca, cb):
    return lax.dot_general(
        a, b, (((ca,), (cb,)), ((), ())), precision=HIGHEST, preferred_element_type=F32
    )


def halves(a):
    high = a.astype(jnp.bfloat16)
    return high, (a - high.astype(F32)).astype(jnp.bfloat16)


def dot3(a, b, ca, cb):
    ah, al = halves(a)
    bh, bl = halves(b)
    one = lambda x, y: lax.dot_general(x, y, (((ca,), (cb,)), ((), ())), preferred_element_type=F32)
    return one(ah, bh) + (one(ah, bl) + one(al, bh))


def vmem(n):
    return [pl.BlockSpec(memory_space=pltpu.VMEM)] * n


def hbm(n):
    return [pl.BlockSpec(memory_space=pltpu.HBM)] * n


class Place:
    def __init__(self, R, F, T):
        self.R, self.F, self.T, self.n = R, F, T, R * T
        self.r = lax.axis_index("replica")
        self.f = lax.axis_index("fsdp")
        self.t = lax.axis_index("tensor")
        self.p = self.r * T + self.t

    def plane(self, d):
        q = lax.rem(self.p + d, self.n)
        return q, {"replica": q // self.T, "tensor": lax.rem(q, self.T)}

    def plane_from(self, d):
        return lax.rem(self.p + self.n - d, self.n)

    def line(self, d):
        q = lax.rem(self.f + d, self.F)
        return q, {"fsdp": q}

    def line_from(self, d):
        return lax.rem(self.f + self.F - d, self.F)

    def cross(self):
        low = lax.rem(self.r, 2)
        return self.r + 1 - 2 * low, lax.rem(self.r + 2, 4), 3 - self.r

    def rep(self, d):
        q = lax.rem(self.r + d, self.R)
        return q, {"replica": q}

    def rep_from(self, d):
        return lax.rem(self.r + self.R - d, self.R)


def remote(src, dst, send, recv, where):
    return pltpu.make_async_remote_copy(
        src_ref=src, dst_ref=dst, send_sem=send, recv_sem=recv, device_id=where, device_id_type=MESH
    )


def greet(targets):
    barrier = pltpu.get_barrier_semaphore()
    for where in targets:
        pl.semaphore_signal(barrier, inc=1, device_id=where, device_id_type=MESH)
    pl.semaphore_wait(barrier, len(targets))


def pack(part):
    rows, share = part.shape
    whole = share // 128 * 128
    tiles = [part[:, i:i + 128] for i in range(0, whole, 128)]
    if whole < share:
        half = rows // 2
        tiles.append(jnp.concatenate([part[:half, whole:], part[half:, whole:]], axis=1))
    return jnp.concatenate(tiles, axis=0)


def unpack(flat, rows, share):
    whole = share // 128 * 128
    tiles = [flat[i * rows:(i + 1) * rows] for i in range(whole // 128)]
    if whole < share:
        last = flat[whole // 128 * rows:]
        tiles.append(jnp.concatenate([last[:, :64], last[:, 64:]], axis=0))
    return jnp.concatenate(tiles, axis=1)


def project_kernel(
    R, F, T, mom_in, grad_in, q_in, bmean_out, proj_out,
    mom, grad, bufs, brecv, qs, pp, precv, proj,
    in_sem, q_sem, b_send, b_recv, q_up, q_down, q_recv, p_send, p_recv, a_send, a_recv,
):
    at = Place(R, F, T)
    rows, cols = mom.shape
    share = cols // R
    n = at.n
    loads = [
        pltpu.make_async_copy(mom_in.at[0], mom, in_sem.at[0]),
        pltpu.make_async_copy(grad_in.at[0], grad, in_sem.at[1]),
    ]
    for copy in loads:
        copy.start()
    nb = F // R
    nc, qc = qs.shape[1], qs.shape[2]

    def fetch(j, c):
        return pltpu.make_async_copy(q_in.at[pl.ds(c * qc, qc)], qs.at[j, c], q_sem.at[j, c])

    for j in range(nb):
        @pl.when(at.f == at.r * nb + j)
        def _():
            for c in range(nc):
                fetch(j, c).start()

    greet([at.plane(d)[1] for d in range(1, n)] + [at.line(d)[1] for d in range(1, F)])

    for copy in loads:
        copy.wait()
    half = bufs.shape[2]
    for k in range(R):
        part = slice(k * share, (k + 1) * share)
        flat = pack(mom[:, part] + grad[:, part].astype(F32))
        for h in range(2):
            bufs[k, h] = flat[h * half:(h + 1) * half]

    rx, ry, rd = at.cross()
    sent = []

    def hop(src, h, slot, k):
        return remote(bufs.at[src, h], brecv.at[h, slot], b_send.at[h, slot], b_recv.at[h, slot], {"replica": k})

    for slot in range(2):
        for h, first in enumerate((rx, ry)):
            copy = hop((rd, first)[slot], h, slot, first)
            copy.start()
            sent.append(copy)

    def up(j, c):
        return remote(qs.at[j, c], qs.at[j, c], q_up.at[j, c], q_recv.at[j, c], {"fsdp": lax.rem(at.f + 1, F)})

    def down(j, c):
        return remote(qs.at[j, c], qs.at[j, c], q_down.at[j, c], q_recv.at[j, c], {"fsdp": lax.rem(at.f + F - 1, F)})

    def pass_on(c, j):
        home = at.r * nb + j
        @pl.when(at.f == home)
        def _():
            fetch(j, c).wait()
        @pl.when(at.f != home)
        def _():
            up(j, c).wait_recv()
        @pl.when((at.f >= home) & (at.f < F - 1))
        def _():
            up(j, c).start()
        @pl.when((at.f <= home) & (at.f > 0))
        def _():
            down(j, c).start()

    for c in range(nc):
        for j in range(nb):
            pass_on(c, j)
        if c == 0:
            for h, second in enumerate((ry, rx)):
                hop(rd, h, 0, second).wait_recv()
                bufs[second, h] = bufs[second, h] + brecv[h, 0]
                copy = hop(second, h, 2, second)
                copy.start()
                sent.append(copy)
    for h, (first, second) in enumerate(((rx, ry), (ry, rx))):
        hop(first, h, 1, first).wait_recv()
    for h, second in enumerate((ry, rx)):
        hop(second, h, 2, second).wait_recv()
    flat = jnp.concatenate([bufs[at.r, h] + brecv[h, 1] + brecv[h, 2] for h in range(2)], axis=0)
    bmean = unpack(flat * (1.0 / R), rows, share)
    bmean_out[...] = bmean
    part = dot(bmean, qs[...].reshape(share, q_in.shape[1]), 1, 0)
    pp[...] = part.reshape(pp.shape)

    for d in range(1, n):
        q, where = at.plane(d)
        copy = remote(pp.at[q], precv.at[at.p], p_send.at[d - 1], p_recv.at[at.p], where)
        copy.start()
        sent.append(copy)
    precv[at.p] = pp[at.p]
    for d in range(1, n):
        q = at.plane_from(d)
        remote(pp.at[q], precv.at[q], p_send.at[d - 1], p_recv.at[q], at.plane(d)[1]).wait_recv()
    total = precv[0]
    for k in range(1, n):
        total = total + precv[k]
    proj[at.p] = total
    for d in range(1, n):
        q, where = at.plane(d)
        copy = remote(proj.at[at.p], proj.at[at.p], a_send.at[d - 1], a_recv.at[at.p], where)
        copy.start()
        sent.append(copy)
    for d in range(1, n):
        q = at.plane_from(d)
        remote(proj.at[q], proj.at[q], a_send.at[d - 1], a_recv.at[q], at.plane(d)[1]).wait_recv()
    whole = proj[...].reshape(rows, q_in.shape[1])
    proj_out[...] = whole

    for copy in sent:
        copy.wait_send()
    for c in range(nc):
        for j in range(nb):
            home = at.r * nb + j
            @pl.when((at.f >= home) & (at.f < F - 1))
            def _():
                up(j, c).wait_send()
            @pl.when((at.f <= home) & (at.f > 0))
            def _():
                down(j, c).wait_send()


def eliminate(tile, side):
    b = tile.shape[0]
    rows_id = lax.broadcasted_iota(jnp.int32, tile.shape, 0)
    lanes = lax.broadcasted_iota(jnp.int32, tile.shape, 1)
    other = b - side
    inside = (lanes >= side) & (lanes < side + b)
    x = jnp.where(inside, tile, jnp.where(lanes - other == rows_id, 1.0, 0.0).astype(F32))
    done = []
    for k0 in range(0, b, 8):
        shape = x.shape
        ids = lax.broadcasted_iota(jnp.int32, shape, 0)
        panel = [
            jnp.broadcast_to(x[:, side + k0 + j:side + k0 + j + 1], shape) for j in range(8)
        ]
        for j in range(8):
            inverse = 1.0 / panel[j][j:j + 1, :]
            scale = jnp.where(ids > j, panel[j], 0.0) * inverse
            for i in range(j + 1, 8):
                panel[i] = panel[i] - scale * panel[i][j:j + 1, :]
            x = x - scale * x[j:j + 1, :]
        done.append(x[:8])
        x = x[8:]
    x = jnp.concatenate(done, axis=0)
    pivot = jnp.sum(jnp.where(lanes - side == rows_id, x, 0.0), axis=1, keepdims=True)
    return x * (1.0 / jnp.sqrt(pivot))


def factor_step(w, o, b):
    size = w.shape[0]
    base = o // 128 * 128
    side = o - base
    x = eliminate(w[o:o + b, base:base + 128], side)
    block = w[o:o + b, :]
    zero = jnp.zeros_like(block)
    stack = jnp.concatenate([zero, block] if side == 0 else [block, zero], axis=0)
    strip = dot(x, stack, 1, 0)
    w[o:o + b, :] = strip
    if o + b < size:
        update = dot(strip[:, :size], strip, 0, 0)
        w[o + b:, :] = w[o + b:, :] - update[o + b:, :]


def back_kernel(
    R, F, T, mom_in, grad_in, bmean, proj, left_out, right_out, mom_out,
    mom, grad, gp, grecv, gram, w, bp, zrecv, full, sq, sqrecv,
    in_sem, g_send, g_recv, h_send, h_recv,
    z_send, z_recv, a_send, a_recv, r_send, r_recv, s_send, s_recv,
):
    at = Place(R, F, T)
    n = at.n
    loads = [
        pltpu.make_async_copy(mom_in.at[0], mom, in_sem.at[0]),
        pltpu.make_async_copy(grad_in.at[0], grad, in_sem.at[1]),
    ]
    for copy in loads:
        copy.start()
    rows, cols = mom.shape
    piece = bp.shape[1]
    rank = proj.shape[1]
    tens = [{"tensor": lax.rem(at.t + d, T)} for d in range(1, T)]
    sent = []

    def go(copy):
        copy.start()
        sent.append(copy)

    whole = proj[...]
    gp[...] = dot(whole, whole, 0, 0).reshape(gp.shape)
    greet([at.plane(d)[1] for d in range(1, n)] + [at.line(d)[1] for d in range(1, F)])
    for d in range(1, F):
        q, where = at.line(d)
        go(remote(gp.at[at.p], grecv.at[at.f], g_send.at[d - 1], g_recv.at[at.f], where))
    grecv[at.f] = gp[at.p]

    back = dot(bmean[...], whole, 0, 0)
    for g in range(F):
        bp[g] = back[g * piece:(g + 1) * piece, :]
    for d in range(1, F):
        q, where = at.line(d)
        go(remote(bp.at[q], zrecv.at[at.f], z_send.at[d - 1], z_recv.at[at.f], where))
    zrecv[at.f] = bp[at.f]

    for d in range(1, F):
        q = at.line_from(d)
        remote(gp.at[at.p], grecv.at[q], g_send.at[d - 1], g_recv.at[q], at.line(d)[1]).wait_recv()
    total = grecv[0]
    for k in range(1, F):
        total = total + grecv[k]
    gram[at.p] = total
    for d in range(1, n):
        q, where = at.plane(d)
        go(remote(gram.at[at.p], gram.at[at.p], h_send.at[d - 1], h_recv.at[at.p], where))
    for d in range(1, n):
        q = at.plane_from(d)
        remote(gram.at[q], gram.at[q], h_send.at[d - 1], h_recv.at[q], at.plane(d)[1]).wait_recv()
    w[:, :rank] = gram[...].reshape(rank, rank)
    ids = lax.broadcasted_iota(jnp.int32, (rank, rank), 0)
    lanes = lax.broadcasted_iota(jnp.int32, (rank, rank), 1)
    w[:, rank:] = jnp.where(ids == lanes, 1.0, 0.0).astype(F32)

    def forward(f, i):
        for d in range(1, R):
            q, where = at.rep(d)
            go(remote(full.at[at.r, f], full.at[at.r, f], r_send.at[i, d - 1], r_recv.at[at.r, f], where))

    def reduced():
        for d in range(1, F):
            q = at.line_from(d)
            remote(bp.at[q], zrecv.at[q], z_send.at[d - 1], z_recv.at[q], at.line(d)[1]).wait_recv()
        total = zrecv[0]
        for k in range(1, F):
            total = total + zrecv[k]
        full[at.r, at.f] = total
        for d in range(1, F):
            q, where = at.line(d)
            go(remote(full.at[at.r, at.f], full.at[at.r, at.f], a_send.at[d - 1], a_recv.at[at.f], where))
        forward(at.f, 0)

    def gathered(d):
        q = at.line_from(d)
        remote(full.at[at.r, q], full.at[at.r, q], a_send.at[d - 1], a_recv.at[q], at.line(d)[1]).wait_recv()
        forward(q, d)

    reduced()
    b = 64
    moves = [lambda d=d: gathered(d) for d in range(1, F)]
    steps = rank // b
    for i in range(steps):
        factor_step(w, i * b, b)
        due = len(moves) * (i + 1) // (steps - 1) - len(moves) * i // (steps - 1) if i < steps - 1 else 0
        first = len(moves) * i // (steps - 1)
        for m in moves[first:first + due]:
            m()
    inverse = w[:, rank:]
    ortho = dot(whole, inverse, 1, 1)
    left_out[...] = ortho * math.sqrt(rows * F)
    for i in range(F):
        g = at.line_from(i)
        for d in range(1, R):
            k = at.rep_from(d)
            remote(full.at[k, g], full.at[k, g], r_send.at[i, d - 1], r_recv.at[k, g], at.rep(d)[1]).wait_recv()
    for copy in sent:
        copy.wait_send()

    squares = jnp.zeros((1, rank), F32)
    blocks = []
    for m in range(2):
        terms = jnp.concatenate(
            [full[k, g] for k in range(m * R // 2, (m + 1) * R // 2) for g in range(F)], axis=0
        )
        v = dot(terms, inverse, 1, 1)
        squares = squares + jnp.sum(v * v, axis=0, keepdims=True)
        count = R * F // 2
        for i in range(count):
            j = m * count + i
            full[j // F, j % F] = v[i * piece:(i + 1) * piece]
        blocks.append(v)
    sq[...] = jnp.broadcast_to(squares, sq.shape)
    norms = []
    for d in range(1, T):
        copy = remote(sq, sqrecv.at[at.t], s_send.at[d - 1], s_recv.at[at.t], tens[d - 1])
        copy.start()
        norms.append(copy)
    sqrecv[at.t] = sq[...]

    for copy in loads:
        copy.wait()
    o = ortho * -0.1
    for m in range(2):
        here = pl.ds(m * (cols // 2), cols // 2)
        mom_out[0, :, here] = mom[:, here] + grad[:, here].astype(F32) + dot3(o, blocks[m], 1, 1)

    for d in range(1, T):
        k = lax.rem(at.t + T - d, T)
        remote(sq, sqrecv.at[k], s_send.at[d - 1], s_recv.at[k], tens[d - 1]).wait_recv()
    total = sqrecv[0]
    for k in range(1, T):
        total = total + sqrecv[k]
    norm = jnp.sqrt(total[0:1, :] + 1e-06)
    scale = math.sqrt(cols * T) / norm
    for i in range(R):
        k = at.f * R + i
        right_out[i * piece:(i + 1) * piece, :] = full[k // F, lax.rem(k, F)] * scale
    for copy in norms:
        copy.wait_send()


def solution(mesh):
    R, F, T = mesh.shape["replica"], mesh.shape["fsdp"], mesh.shape["tensor"]
    n = R * T
    DMA = pltpu.SemaphoreType.DMA

    def shards(momentum, gradient, right_in):
        rows, cols = momentum.shape[1], momentum.shape[2]
        qb, rank = right_in.shape
        share = cols // R
        nb = F // R
        nc = 8 if qb % 64 == 0 else 1
        piece = share // F
        sds = jax.ShapeDtypeStruct
        slots = lambda m, r: pltpu.VMEM((m, r, rank), F32)
        bmean, proj = pl.pallas_call(
            lambda *refs: project_kernel(R, F, T, *refs),
            out_shape=(sds((rows, share), F32), sds((rows, rank), F32)),
            in_specs=hbm(3),
            out_specs=tuple(vmem(2)),
            scratch_shapes=[
                pltpu.VMEM((rows, cols), F32),
                pltpu.VMEM((rows, cols), gradient.dtype),
                pltpu.VMEM((R, 2, rows * share // 256, 128), F32),
                pltpu.VMEM((2, 3, rows * share // 256, 128), F32),
                pltpu.VMEM((nb, nc, qb // nc, rank), F32),
                slots(n, rows // n),
                slots(n, rows // n),
                slots(n, rows // n),
                DMA((2,)), DMA((nb, nc)), DMA((2, 3)), DMA((2, 3)),
                DMA((nb, nc)), DMA((nb, nc)), DMA((nb, nc)),
                DMA((n,)), DMA((n,)), DMA((n,)), DMA((n,)),
            ],
            compiler_params=pltpu.CompilerParams(
                collective_id=0, has_side_effects=True, vmem_limit_bytes=60 << 20
            ),
            name="project",
        )(momentum, gradient, right_in)
        left, right, updated = pl.pallas_call(
            lambda *refs: back_kernel(R, F, T, *refs),
            out_shape=(sds((rows, rank), F32), sds((qb, rank), F32), sds(momentum.shape, F32)),
            in_specs=hbm(2) + vmem(2),
            out_specs=tuple(vmem(3)),
            scratch_shapes=[
                pltpu.VMEM((rows, cols), F32),
                pltpu.VMEM((rows, cols), gradient.dtype),
                slots(n, rank // n),
                slots(F, rank // n),
                slots(n, rank // n),
                pltpu.VMEM((rank, 2 * rank), F32),
                slots(F, piece),
                slots(F, piece),
                pltpu.VMEM((R, F, piece, rank), F32),
                pltpu.VMEM((8, rank), F32),
                slots(T, 8),
                DMA((2,)),
                DMA((F,)), DMA((F,)), DMA((n,)), DMA((n,)),
                DMA((F,)), DMA((F,)), DMA((F,)), DMA((F,)),
                DMA((F, R)), DMA((R, F)), DMA((T,)), DMA((T,)),
            ],
            compiler_params=pltpu.CompilerParams(
                collective_id=1, has_side_effects=True, vmem_limit_bytes=40 << 20
            ),
            name="back",
        )(momentum, gradient, bmean, proj)
        return left, right, updated

    placed = (
        P("replica", "fsdp", "tensor"),
        P("replica", "fsdp", "tensor"),
        P(("tensor", "fsdp"), None),
    )
    return jax.shard_map(
        shards,
        mesh=mesh,
        in_specs=placed,
        out_specs=(P("fsdp", None), P(("tensor", "fsdp"), None), P("replica", "fsdp", "tensor")),
        check_vma=False,
    )
```

```python
import math

import jax
import jax.numpy as jnp
from jax import lax
from jax.experimental import pallas as pl
from jax.experimental.pallas import tpu as pltpu
from jax.sharding import PartitionSpec as P

MESH = pl.DeviceIdType.MESH
HIGHEST = lax.Precision.HIGHEST
F32 = jnp.float32


def dot(a, b, ca, cb):
    return lax.dot_general(
        a, b, (((ca,), (cb,)), ((), ())), precision=HIGHEST, preferred_element_type=F32
    )


def halves(a):
    high = a.astype(jnp.bfloat16)
    return high, (a - high.astype(F32)).astype(jnp.bfloat16)


def dot3(a, b, ca, cb):
    ah, al = halves(a)
    bh, bl = halves(b)
    one = lambda x, y: lax.dot_general(x, y, (((ca,), (cb,)), ((), ())), preferred_element_type=F32)
    return one(ah, bh) + (one(ah, bl) + one(al, bh))


def vmem(n):
    return [pl.BlockSpec(memory_space=pltpu.VMEM)] * n


def hbm(n):
    return [pl.BlockSpec(memory_space=pltpu.HBM)] * n


class Place:
    def __init__(self, R, F, T):
        self.R, self.F, self.T, self.n = R, F, T, R * T
        self.r = lax.axis_index("replica")
        self.f = lax.axis_index("fsdp")
        self.t = lax.axis_index("tensor")
        self.p = self.r * T + self.t

    def plane(self, d):
        q = lax.rem(self.p + d, self.n)
        return q, {"replica": q // self.T, "tensor": lax.rem(q, self.T)}

    def plane_from(self, d):
        return lax.rem(self.p + self.n - d, self.n)

    def line(self, d):
        q = lax.rem(self.f + d, self.F)
        return q, {"fsdp": q}

    def line_from(self, d):
        return lax.rem(self.f + self.F - d, self.F)

    def cross(self):
        low = lax.rem(self.r, 2)
        return self.r + 1 - 2 * low, lax.rem(self.r + 2, 4), 3 - self.r

    def rep(self, d):
        q = lax.rem(self.r + d, self.R)
        return q, {"replica": q}

    def rep_from(self, d):
        return lax.rem(self.r + self.R - d, self.R)


def remote(src, dst, send, recv, where):
    return pltpu.make_async_remote_copy(
        src_ref=src, dst_ref=dst, send_sem=send, recv_sem=recv, device_id=where, device_id_type=MESH
    )


def greet(targets):
    barrier = pltpu.get_barrier_semaphore()
    for where in targets:
        pl.semaphore_signal(barrier, inc=1, device_id=where, device_id_type=MESH)
    pl.semaphore_wait(barrier, len(targets))


def pack(part):
    rows, share = part.shape
    whole = share // 128 * 128
    tiles = [part[:, i:i + 128] for i in range(0, whole, 128)]
    if whole < share:
        half = rows // 2
        tiles.append(jnp.concatenate([part[:half, whole:], part[half:, whole:]], axis=1))
    return jnp.concatenate(tiles, axis=0)


def unpack(flat, rows, share):
    whole = share // 128 * 128
    tiles = [flat[i * rows:(i + 1) * rows] for i in range(whole // 128)]
    if whole < share:
        last = flat[whole // 128 * rows:]
        tiles.append(jnp.concatenate([last[:, :64], last[:, 64:]], axis=0))
    return jnp.concatenate(tiles, axis=1)


def project_kernel(
    R, F, T, mom_in, grad_in, q_in, bmean_out, proj_out,
    mom, grad, bufs, brecv, qs, pp, precv, proj,
    in_sem, q_sem, b_send, b_recv, q_up, q_down, q_recv, p_send, p_recv, a_send, a_recv,
):
    at = Place(R, F, T)
    rows, cols = mom.shape
    share = cols // R
    n = at.n
    loads = [
        pltpu.make_async_copy(mom_in.at[0], mom, in_sem.at[0]),
        pltpu.make_async_copy(grad_in.at[0], grad, in_sem.at[1]),
    ]
    for copy in loads:
        copy.start()
    nb = F // R
    nc, qc = qs.shape[1], qs.shape[2]

    def fetch(j, c):
        return pltpu.make_async_copy(q_in.at[pl.ds(c * qc, qc)], qs.at[j, c], q_sem.at[j, c])

    for j in range(nb):
        @pl.when(at.f == at.r * nb + j)
        def _():
            for c in range(nc):
                fetch(j, c).start()

    greet([at.plane(d)[1] for d in range(1, n)] + [at.line(d)[1] for d in range(1, F)])

    for copy in loads:
        copy.wait()
    half = bufs.shape[2]
    for k in range(R):
        part = slice(k * share, (k + 1) * share)
        flat = pack(mom[:, part] + grad[:, part].astype(F32))
        for h in range(2):
            bufs[k, h] = flat[h * half:(h + 1) * half]

    rx, ry, rd = at.cross()
    sent = []

    def hop(src, h, slot, k):
        return remote(bufs.at[src, h], brecv.at[h, slot], b_send.at[h, slot], b_recv.at[h, slot], {"replica": k})

    for slot in range(2):
        for h, first in enumerate((rx, ry)):
            copy = hop((rd, first)[slot], h, slot, first)
            copy.start()
            sent.append(copy)

    def up(j, c):
        return remote(qs.at[j, c], qs.at[j, c], q_up.at[j, c], q_recv.at[j, c], {"fsdp": lax.rem(at.f + 1, F)})

    def down(j, c):
        return remote(qs.at[j, c], qs.at[j, c], q_down.at[j, c], q_recv.at[j, c], {"fsdp": lax.rem(at.f + F - 1, F)})

    def pass_on(c, j):
        home = at.r * nb + j
        @pl.when(at.f == home)
        def _():
            fetch(j, c).wait()
        @pl.when(at.f != home)
        def _():
            up(j, c).wait_recv()
        @pl.when((at.f >= home) & (at.f < F - 1))
        def _():
            up(j, c).start()
        @pl.when((at.f <= home) & (at.f > 0))
        def _():
            down(j, c).start()

    for c in range(nc):
        for j in range(nb):
            pass_on(c, j)
        if c == 0:
            for h, second in enumerate((ry, rx)):
                hop(rd, h, 0, second).wait_recv()
                bufs[second, h] = bufs[second, h] + brecv[h, 0]
                copy = hop(second, h, 2, second)
                copy.start()
                sent.append(copy)
    for h, (first, second) in enumerate(((rx, ry), (ry, rx))):
        hop(first, h, 1, first).wait_recv()
    for h, second in enumerate((ry, rx)):
        hop(second, h, 2, second).wait_recv()
    flat = jnp.concatenate([bufs[at.r, h] + brecv[h, 1] + brecv[h, 2] for h in range(2)], axis=0)
    bmean = unpack(flat * (1.0 / R), rows, share)
    bmean_out[...] = bmean
    part = dot(bmean, qs[...].reshape(share, q_in.shape[1]), 1, 0)
    pp[...] = part.reshape(pp.shape)

    for d in range(1, n):
        q, where = at.plane(d)
        copy = remote(pp.at[q], precv.at[at.p], p_send.at[d - 1], p_recv.at[at.p], where)
        copy.start()
        sent.append(copy)
    precv[at.p] = pp[at.p]
    for d in range(1, n):
        q = at.plane_from(d)
        remote(pp.at[q], precv.at[q], p_send.at[d - 1], p_recv.at[q], at.plane(d)[1]).wait_recv()
    total = precv[0]
    for k in range(1, n):
        total = total + precv[k]
    proj[at.p] = total
    for d in range(1, n):
        q, where = at.plane(d)
        copy = remote(proj.at[at.p], proj.at[at.p], a_send.at[d - 1], a_recv.at[at.p], where)
        copy.start()
        sent.append(copy)
    for d in range(1, n):
        q = at.plane_from(d)
        remote(proj.at[q], proj.at[q], a_send.at[d - 1], a_recv.at[q], at.plane(d)[1]).wait_recv()
    whole = proj[...].reshape(rows, q_in.shape[1])
    proj_out[...] = whole

    for copy in sent:
        copy.wait_send()
    for c in range(nc):
        for j in range(nb):
            home = at.r * nb + j
            @pl.when((at.f >= home) & (at.f < F - 1))
            def _():
                up(j, c).wait_send()
            @pl.when((at.f <= home) & (at.f > 0))
            def _():
                down(j, c).wait_send()


def eliminate(tile, side):
    b = tile.shape[0]
    rows_id = lax.broadcasted_iota(jnp.int32, tile.shape, 0)
    lanes = lax.broadcasted_iota(jnp.int32, tile.shape, 1)
    other = b - side
    inside = (lanes >= side) & (lanes < side + b)
    x = jnp.where(inside, tile, jnp.where(lanes - other == rows_id, 1.0, 0.0).astype(F32))
    done = []
    for k0 in range(0, b, 8):
        shape = x.shape
        ids = lax.broadcasted_iota(jnp.int32, shape, 0)
        panel = [
            jnp.broadcast_to(x[:, side + k0 + j:side + k0 + j + 1], shape) for j in range(8)
        ]
        for j in range(8):
            inverse = 1.0 / panel[j][j:j + 1, :]
            scale = jnp.where(ids > j, panel[j], 0.0) * inverse
            for i in range(j + 1, 8):
                panel[i] = panel[i] - scale * panel[i][j:j + 1, :]
            x = x - scale * x[j:j + 1, :]
        done.append(x[:8])
        x = x[8:]
    x = jnp.concatenate(done, axis=0)
    pivot = jnp.sum(jnp.where(lanes - side == rows_id, x, 0.0), axis=1, keepdims=True)
    return x * (1.0 / jnp.sqrt(pivot))


def factor_step(w, o, b):
    size = w.shape[0]
    base = o // 128 * 128
    side = o - base
    x = eliminate(w[o:o + b, base:base + 128], side)
    block = w[o:o + b, :]
    zero = jnp.zeros_like(block)
    stack = jnp.concatenate([zero, block] if side == 0 else [block, zero], axis=0)
    strip = dot(x, stack, 1, 0)
    w[o:o + b, :] = strip
    if o + b < size:
        update = dot(strip[:, :size], strip, 0, 0)
        w[o + b:, :] = w[o + b:, :] - update[o + b:, :]


def back_kernel(
    R, F, T, mom_in, grad_in, bmean, proj, left_out, right_out, mom_out,
    mom, grad, gp, grecv, gram, w, bp, zrecv, full, final, sq, sqrecv,
    in_sem, g_send, g_recv, h_send, h_recv,
    z_send, z_recv, a_send, a_recv, r_send, r_recv, s_send, s_recv,
):
    at = Place(R, F, T)
    n = at.n
    loads = [
        pltpu.make_async_copy(mom_in.at[0], mom, in_sem.at[0]),
        pltpu.make_async_copy(grad_in.at[0], grad, in_sem.at[1]),
    ]
    for copy in loads:
        copy.start()
    rows, cols = mom.shape
    piece = bp.shape[1]
    rank = proj.shape[1]
    tens = [{"tensor": lax.rem(at.t + d, T)} for d in range(1, T)]
    sent = []

    def go(copy):
        copy.start()
        sent.append(copy)

    whole = proj[...]
    gp[...] = dot(whole, whole, 0, 0).reshape(gp.shape)
    back = dot(bmean[...], whole, 0, 0)
    for g in range(F):
        bp[g] = back[g * piece:(g + 1) * piece, :]
    greet([at.plane(d)[1] for d in range(1, n)] + [at.line(d)[1] for d in range(1, F)])
    for d in range(1, F):
        q, where = at.line(d)
        go(remote(gp.at[at.p], grecv.at[at.f], g_send.at[d - 1], g_recv.at[at.f], where))
    grecv[at.f] = gp[at.p]

    for d in range(1, F):
        q, where = at.line(d)
        go(remote(bp.at[q], zrecv.at[at.f], z_send.at[d - 1], z_recv.at[at.f], where))
    zrecv[at.f] = bp[at.f]

    for d in range(1, F):
        q = at.line_from(d)
        remote(gp.at[at.p], grecv.at[q], g_send.at[d - 1], g_recv.at[q], at.line(d)[1]).wait_recv()
    total = grecv[0]
    for k in range(1, F):
        total = total + grecv[k]
    gram[at.p] = total
    for d in range(1, n):
        q, where = at.plane(d)
        go(remote(gram.at[at.p], gram.at[at.p], h_send.at[d - 1], h_recv.at[at.p], where))

    def forward(f, i):
        for d in range(1, R):
            q, where = at.rep(d)
            go(remote(full.at[at.r, f], full.at[at.r, f], r_send.at[i, d - 1], r_recv.at[at.r, f], where))

    def reduced():
        for d in range(1, F):
            q = at.line_from(d)
            remote(bp.at[q], zrecv.at[q], z_send.at[d - 1], z_recv.at[q], at.line(d)[1]).wait_recv()
        total = zrecv[0]
        for k in range(1, F):
            total = total + zrecv[k]
        full[at.r, at.f] = total
        for d in range(1, F):
            q, where = at.line(d)
            go(remote(full.at[at.r, at.f], full.at[at.r, at.f], a_send.at[d - 1], a_recv.at[at.f], where))
        forward(at.f, 0)

    def gathered(d):
        q = at.line_from(d)
        remote(full.at[at.r, q], full.at[at.r, q], a_send.at[d - 1], a_recv.at[q], at.line(d)[1]).wait_recv()
        forward(q, d)

    reduced()
    for d in range(1, n):
        q = at.plane_from(d)
        remote(gram.at[q], gram.at[q], h_send.at[d - 1], h_recv.at[q], at.plane(d)[1]).wait_recv()
    w[:, :rank] = gram[...].reshape(rank, rank)
    ids = lax.broadcasted_iota(jnp.int32, (rank, rank), 0)
    lanes = lax.broadcasted_iota(jnp.int32, (rank, rank), 1)
    w[:, rank:] = jnp.where(ids == lanes, 1.0, 0.0).astype(F32)
    b = 64
    steps = rank // b
    later = steps // 2
    moved = 1
    for i in range(steps):
        factor_step(w, i * b, b)
        if later <= i + 1 < steps:
            until = F if i + 2 == steps else moved + max(1, (F - 1) // (steps - later))
            for d in range(moved, min(until, F)):
                gathered(d)
            moved = min(until, F)
    inverse = w[:, rank:]
    ortho = dot(whole, inverse, 1, 1)
    left_out[...] = ortho * math.sqrt(rows * F)
    squares = jnp.zeros((1, rank), F32)
    for i in range(F):
        g = at.line_from(i)
        for d in range(1, R):
            k = at.rep_from(d)
            remote(full.at[k, g], full.at[k, g], r_send.at[i, d - 1], r_recv.at[k, g], at.rep(d)[1]).wait_recv()
        v = dot(jnp.concatenate([full[k, g] for k in range(R)], axis=0), inverse, 1, 1)
        squares = squares + jnp.sum(v * v, axis=0, keepdims=True)
        for k in range(R):
            final[k, g] = v[k * piece:(k + 1) * piece]
    sq[...] = jnp.broadcast_to(squares, sq.shape)
    norms = []
    for d in range(1, T):
        copy = remote(sq, sqrecv.at[at.t], s_send.at[d - 1], s_recv.at[at.t], tens[d - 1])
        copy.start()
        norms.append(copy)
    sqrecv[at.t] = sq[...]

    for copy in loads:
        copy.wait()
    o = ortho * -0.1
    for m in range(2):
        here = pl.ds(m * (cols // 2), cols // 2)
        block = jnp.concatenate(
            [final[k, g] for k in range(m * R // 2, (m + 1) * R // 2) for g in range(F)], axis=0
        )
        mom_out[0, :, here] = mom[:, here] + grad[:, here].astype(F32) + dot3(o, block, 1, 1)

    for d in range(1, T):
        k = lax.rem(at.t + T - d, T)
        remote(sq, sqrecv.at[k], s_send.at[d - 1], s_recv.at[k], tens[d - 1]).wait_recv()
    total = sqrecv[0]
    for k in range(1, T):
        total = total + sqrecv[k]
    norm = jnp.sqrt(total[0:1, :] + 1e-06)
    scale = math.sqrt(cols * T) / norm
    for i in range(R):
        k = at.f * R + i
        right_out[i * piece:(i + 1) * piece, :] = final[k // F, lax.rem(k, F)] * scale
    for copy in sent + norms:
        copy.wait_send()


def solution(mesh):
    R, F, T = mesh.shape["replica"], mesh.shape["fsdp"], mesh.shape["tensor"]
    n = R * T
    DMA = pltpu.SemaphoreType.DMA

    def shards(momentum, gradient, right_in):
        rows, cols = momentum.shape[1], momentum.shape[2]
        qb, rank = right_in.shape
        share = cols // R
        nb = F // R
        nc = 8 if qb % 64 == 0 else 1
        piece = share // F
        sds = jax.ShapeDtypeStruct
        slots = lambda m, r: pltpu.VMEM((m, r, rank), F32)
        bmean, proj = pl.pallas_call(
            lambda *refs: project_kernel(R, F, T, *refs),
            out_shape=(sds((rows, share), F32), sds((rows, rank), F32)),
            in_specs=hbm(3),
            out_specs=tuple(vmem(2)),
            scratch_shapes=[
                pltpu.VMEM((rows, cols), F32),
                pltpu.VMEM((rows, cols), gradient.dtype),
                pltpu.VMEM((R, 2, rows * share // 256, 128), F32),
                pltpu.VMEM((2, 3, rows * share // 256, 128), F32),
                pltpu.VMEM((nb, nc, qb // nc, rank), F32),
                slots(n, rows // n),
                slots(n, rows // n),
                slots(n, rows // n),
                DMA((2,)), DMA((nb, nc)), DMA((2, 3)), DMA((2, 3)),
                DMA((nb, nc)), DMA((nb, nc)), DMA((nb, nc)),
                DMA((n,)), DMA((n,)), DMA((n,)), DMA((n,)),
            ],
            compiler_params=pltpu.CompilerParams(
                collective_id=0, has_side_effects=True, vmem_limit_bytes=60 << 20
            ),
            name="project",
        )(momentum, gradient, right_in)
        left, right, updated = pl.pallas_call(
            lambda *refs: back_kernel(R, F, T, *refs),
            out_shape=(sds((rows, rank), F32), sds((qb, rank), F32), sds(momentum.shape, F32)),
            in_specs=hbm(2) + vmem(2),
            out_specs=tuple(vmem(3)),
            scratch_shapes=[
                pltpu.VMEM((rows, cols), F32),
                pltpu.VMEM((rows, cols), gradient.dtype),
                slots(n, rank // n),
                slots(F, rank // n),
                slots(n, rank // n),
                pltpu.VMEM((rank, 2 * rank), F32),
                slots(F, piece),
                slots(F, piece),
                pltpu.VMEM((R, F, piece, rank), F32),
                pltpu.VMEM((R, F, piece, rank), F32),
                pltpu.VMEM((8, rank), F32),
                slots(T, 8),
                DMA((2,)),
                DMA((F,)), DMA((F,)), DMA((n,)), DMA((n,)),
                DMA((F,)), DMA((F,)), DMA((F,)), DMA((F,)),
                DMA((F, R)), DMA((R, F)), DMA((T,)), DMA((T,)),
            ],
            compiler_params=pltpu.CompilerParams(
                collective_id=1, has_side_effects=True, vmem_limit_bytes=40 << 20
            ),
            name="back",
        )(momentum, gradient, bmean, proj)
        return left, right, updated

    placed = (
        P("replica", "fsdp", "tensor"),
        P("replica", "fsdp", "tensor"),
        P(("tensor", "fsdp"), None),
    )
    return jax.shard_map(
        shards,
        mesh=mesh,
        in_specs=placed,
        out_specs=(P("fsdp", None), P(("tensor", "fsdp"), None), P("replica", "fsdp", "tensor")),
        check_vma=False,
    )
```

```python
import math

import jax
import jax.numpy as jnp
from jax import lax
from jax.experimental import pallas as pl
from jax.experimental.pallas import tpu as pltpu
from jax.sharding import PartitionSpec as P

MESH = pl.DeviceIdType.MESH
HIGHEST = lax.Precision.HIGHEST
F32 = jnp.float32


def dot(a, b, ca, cb):
    return lax.dot_general(
        a, b, (((ca,), (cb,)), ((), ())), precision=HIGHEST, preferred_element_type=F32
    )


def halves(a):
    high = a.astype(jnp.bfloat16)
    return high, (a - high.astype(F32)).astype(jnp.bfloat16)


def dot3(a, b, ca, cb):
    ah, al = halves(a)
    bh, bl = halves(b)
    one = lambda x, y: lax.dot_general(x, y, (((ca,), (cb,)), ((), ())), preferred_element_type=F32)
    return one(ah, bh) + (one(ah, bl) + one(al, bh))


def vmem(n):
    return [pl.BlockSpec(memory_space=pltpu.VMEM)] * n


def hbm(n):
    return [pl.BlockSpec(memory_space=pltpu.HBM)] * n


class Place:
    def __init__(self, R, F, T):
        self.R, self.F, self.T, self.n = R, F, T, R * T
        self.r = lax.axis_index("replica")
        self.f = lax.axis_index("fsdp")
        self.t = lax.axis_index("tensor")
        self.p = self.r * T + self.t

    def plane(self, d):
        q = lax.rem(self.p + d, self.n)
        return q, {"replica": q // self.T, "tensor": lax.rem(q, self.T)}

    def plane_from(self, d):
        return lax.rem(self.p + self.n - d, self.n)

    def line(self, d):
        q = lax.rem(self.f + d, self.F)
        return q, {"fsdp": q}

    def line_from(self, d):
        return lax.rem(self.f + self.F - d, self.F)

    def cross(self):
        low = lax.rem(self.r, 2)
        return self.r + 1 - 2 * low, lax.rem(self.r + 2, 4), 3 - self.r

    def rep(self, d):
        q = lax.rem(self.r + d, self.R)
        return q, {"replica": q}

    def rep_from(self, d):
        return lax.rem(self.r + self.R - d, self.R)


def remote(src, dst, send, recv, where):
    return pltpu.make_async_remote_copy(
        src_ref=src, dst_ref=dst, send_sem=send, recv_sem=recv, device_id=where, device_id_type=MESH
    )


def greet(targets):
    barrier = pltpu.get_barrier_semaphore()
    for where in targets:
        pl.semaphore_signal(barrier, inc=1, device_id=where, device_id_type=MESH)
    pl.semaphore_wait(barrier, len(targets))


def pack(part):
    rows, share = part.shape
    whole = share // 128 * 128
    tiles = [part[:, i:i + 128] for i in range(0, whole, 128)]
    if whole < share:
        half = rows // 2
        tiles.append(jnp.concatenate([part[:half, whole:], part[half:, whole:]], axis=1))
    return jnp.concatenate(tiles, axis=0)


def unpack(flat, rows, share):
    whole = share // 128 * 128
    tiles = [flat[i * rows:(i + 1) * rows] for i in range(whole // 128)]
    if whole < share:
        last = flat[whole // 128 * rows:]
        tiles.append(jnp.concatenate([last[:, :64], last[:, 64:]], axis=0))
    return jnp.concatenate(tiles, axis=1)


def project_kernel(
    R, F, T, mom_in, grad_in, q_in, bmean_out, proj_out,
    mom, grad, bufs, brecv, qs, pp, precv, proj,
    in_sem, q_sem, b_send, b_recv, q_up, q_down, q_recv, p_send, p_recv, a_send, a_recv,
):
    at = Place(R, F, T)
    rows, cols = mom.shape
    share = cols // R
    n = at.n
    loads = [
        pltpu.make_async_copy(mom_in.at[0], mom, in_sem.at[0]),
        pltpu.make_async_copy(grad_in.at[0], grad, in_sem.at[1]),
    ]
    for copy in loads:
        copy.start()
    nb = F // R
    nc, qc = qs.shape[1], qs.shape[2]

    def fetch(j, c):
        return pltpu.make_async_copy(q_in.at[pl.ds(c * qc, qc)], qs.at[j, c], q_sem.at[j, c])

    for j in range(nb):
        @pl.when(at.f == at.r * nb + j)
        def _():
            for c in range(nc):
                fetch(j, c).start()

    greet([at.plane(d)[1] for d in range(1, n)] + [at.line(d)[1] for d in range(1, F)])

    for copy in loads:
        copy.wait()
    half = bufs.shape[2]
    for k in range(R):
        part = slice(k * share, (k + 1) * share)
        flat = pack(mom[:, part] + grad[:, part].astype(F32))
        for h in range(2):
            bufs[k, h] = flat[h * half:(h + 1) * half]

    rx, ry, rd = at.cross()
    sent = []

    def hop(src, h, slot, k):
        return remote(bufs.at[src, h], brecv.at[h, slot], b_send.at[h, slot], b_recv.at[h, slot], {"replica": k})

    for slot in range(2):
        for h, first in enumerate((rx, ry)):
            copy = hop((rd, first)[slot], h, slot, first)
            copy.start()
            sent.append(copy)

    def up(j, c):
        return remote(qs.at[j, c], qs.at[j, c], q_up.at[j, c], q_recv.at[j, c], {"fsdp": lax.rem(at.f + 1, F)})

    def down(j, c):
        return remote(qs.at[j, c], qs.at[j, c], q_down.at[j, c], q_recv.at[j, c], {"fsdp": lax.rem(at.f + F - 1, F)})

    def pass_on(c, j):
        home = at.r * nb + j
        @pl.when(at.f == home)
        def _():
            fetch(j, c).wait()
        @pl.when(at.f != home)
        def _():
            up(j, c).wait_recv()
        @pl.when((at.f >= home) & (at.f < F - 1))
        def _():
            up(j, c).start()
        @pl.when((at.f <= home) & (at.f > 0))
        def _():
            down(j, c).start()

    for c in range(nc):
        for j in range(nb):
            pass_on(c, j)
        if c == 0:
            for h, second in enumerate((ry, rx)):
                hop(rd, h, 0, second).wait_recv()
                bufs[second, h] = bufs[second, h] + brecv[h, 0]
                copy = hop(second, h, 2, second)
                copy.start()
                sent.append(copy)
    for h, (first, second) in enumerate(((rx, ry), (ry, rx))):
        hop(first, h, 1, first).wait_recv()
    for h, second in enumerate((ry, rx)):
        hop(second, h, 2, second).wait_recv()
    flat = jnp.concatenate([bufs[at.r, h] + brecv[h, 1] + brecv[h, 2] for h in range(2)], axis=0)
    bmean = unpack(flat * (1.0 / R), rows, share)
    bmean_out[...] = bmean
    part = dot(bmean, qs[...].reshape(share, q_in.shape[1]), 1, 0)
    pp[...] = part.reshape(pp.shape)

    for d in range(1, n):
        q, where = at.plane(d)
        copy = remote(pp.at[q], precv.at[at.p], p_send.at[d - 1], p_recv.at[at.p], where)
        copy.start()
        sent.append(copy)
    precv[at.p] = pp[at.p]
    for d in range(1, n):
        q = at.plane_from(d)
        remote(pp.at[q], precv.at[q], p_send.at[d - 1], p_recv.at[q], at.plane(d)[1]).wait_recv()
    total = precv[0]
    for k in range(1, n):
        total = total + precv[k]
    proj[at.p] = total
    for d in range(1, n):
        q, where = at.plane(d)
        copy = remote(proj.at[at.p], proj.at[at.p], a_send.at[d - 1], a_recv.at[at.p], where)
        copy.start()
        sent.append(copy)
    for d in range(1, n):
        q = at.plane_from(d)
        remote(proj.at[q], proj.at[q], a_send.at[d - 1], a_recv.at[q], at.plane(d)[1]).wait_recv()
    whole = proj[...].reshape(rows, q_in.shape[1])
    proj_out[...] = whole

    for copy in sent:
        copy.wait_send()
    for c in range(nc):
        for j in range(nb):
            home = at.r * nb + j
            @pl.when((at.f >= home) & (at.f < F - 1))
            def _():
                up(j, c).wait_send()
            @pl.when((at.f <= home) & (at.f > 0))
            def _():
                down(j, c).wait_send()


def eliminate(tile, side):
    b = tile.shape[0]
    rows_id = lax.broadcasted_iota(jnp.int32, tile.shape, 0)
    lanes = lax.broadcasted_iota(jnp.int32, tile.shape, 1)
    other = b - side
    inside = (lanes >= side) & (lanes < side + b)
    x = jnp.where(inside, tile, jnp.where(lanes - other == rows_id, 1.0, 0.0).astype(F32))
    done = []
    for k0 in range(0, b, 8):
        shape = x.shape
        ids = lax.broadcasted_iota(jnp.int32, shape, 0)
        panel = [
            jnp.broadcast_to(x[:, side + k0 + j:side + k0 + j + 1], shape) for j in range(8)
        ]
        for j in range(8):
            inverse = 1.0 / panel[j][j:j + 1, :]
            scale = jnp.where(ids > j, panel[j], 0.0) * inverse
            for i in range(j + 1, 8):
                panel[i] = panel[i] - scale * panel[i][j:j + 1, :]
            x = x - scale * x[j:j + 1, :]
        done.append(x[:8])
        x = x[8:]
    x = jnp.concatenate(done, axis=0)
    pivot = jnp.sum(jnp.where(lanes - side == rows_id, x, 0.0), axis=1, keepdims=True)
    return x * (1.0 / jnp.sqrt(pivot))


def factor_step(w, o, b):
    size = w.shape[0]
    base = o // 128 * 128
    side = o - base
    x = eliminate(w[o:o + b, base:base + 128], side)
    block = w[o:o + b, :]
    zero = jnp.zeros_like(block)
    stack = jnp.concatenate([zero, block] if side == 0 else [block, zero], axis=0)
    strip = dot(x, stack, 1, 0)
    w[o:o + b, :] = strip
    if o + b < size:
        update = dot(strip[:, :size], strip, 0, 0)
        w[o + b:, :] = w[o + b:, :] - update[o + b:, :]


def back_kernel(
    R, F, T, mom_in, grad_in, bmean, proj, left_out, right_out, mom_out,
    mom, grad, gp, grecv, gram, w, bp, zrecv, full, final, sq, sqrecv,
    in_sem, g_send, g_recv, h_send, h_recv,
    z_send, z_recv, a_send, a_recv, r_send, r_recv, s_send, s_recv,
):
    at = Place(R, F, T)
    n = at.n
    loads = [
        pltpu.make_async_copy(mom_in.at[0], mom, in_sem.at[0]),
        pltpu.make_async_copy(grad_in.at[0], grad, in_sem.at[1]),
    ]
    for copy in loads:
        copy.start()
    rows, cols = mom.shape
    piece = bp.shape[1]
    rank = proj.shape[1]
    tens = [{"tensor": lax.rem(at.t + d, T)} for d in range(1, T)]
    sent = []

    def go(copy):
        copy.start()
        sent.append(copy)

    rx, ry, rd = at.cross()
    whole = proj[...]
    gp[...] = dot(whole, whole, 0, 0).reshape(gp.shape)
    back = dot(bmean[...], whole, 0, 0)
    for g in range(F):
        bp[g] = back[g * piece:(g + 1) * piece, :]
    greet([at.plane(d)[1] for d in range(1, n)] + [at.line(d)[1] for d in range(1, F)])
    for d in range(1, F):
        q, where = at.line(d)
        go(remote(gp.at[at.p], grecv.at[at.f], g_send.at[d - 1], g_recv.at[at.f], where))
    grecv[at.f] = gp[at.p]

    for d in range(1, F):
        q, where = at.line(d)
        go(remote(bp.at[q], zrecv.at[at.f], z_send.at[d - 1], z_recv.at[at.f], where))
    zrecv[at.f] = bp[at.f]

    for d in range(1, F):
        q = at.line_from(d)
        remote(gp.at[at.p], grecv.at[q], g_send.at[d - 1], g_recv.at[q], at.line(d)[1]).wait_recv()
    total = grecv[0]
    for k in range(1, F):
        total = total + grecv[k]
    gram[at.p] = total
    for d in range(1, n):
        q, where = at.plane(d)
        go(remote(gram.at[at.p], gram.at[at.p], h_send.at[d - 1], h_recv.at[at.p], where))

    def forward(f, i):
        slot = full.at[at.r, f]
        for e, k in enumerate((rx, ry)):
            go(remote(slot, slot, r_send.at[i, e], r_recv.at[at.r, f], {"replica": k}))

    def arrive(k, g):
        slot = full.at[k, g]
        remote(slot, slot, r_send.at[0, 0], r_recv.at[k, g], {"replica": rx}).wait_recv()

    def cross_on(i):
        g = at.line_from(i)
        arrive(rx, g)
        arrive(ry, g)
        odd = lax.rem(g, 2)
        src = rx + (ry - rx) * odd
        slot = full.at[src, g]
        go(remote(slot, slot, r_send.at[i, 2], r_recv.at[src, g], {"replica": ry + (rx - ry) * odd}))

    def reduced():
        for d in range(1, F):
            q = at.line_from(d)
            remote(bp.at[q], zrecv.at[q], z_send.at[d - 1], z_recv.at[q], at.line(d)[1]).wait_recv()
        total = zrecv[0]
        for k in range(1, F):
            total = total + zrecv[k]
        full[at.r, at.f] = total
        for d in range(1, F):
            q, where = at.line(d)
            go(remote(full.at[at.r, at.f], full.at[at.r, at.f], a_send.at[d - 1], a_recv.at[at.f], where))
        forward(at.f, 0)

    def gathered(d):
        q = at.line_from(d)
        remote(full.at[at.r, q], full.at[at.r, q], a_send.at[d - 1], a_recv.at[q], at.line(d)[1]).wait_recv()
        forward(q, d)

    reduced()
    for d in range(1, n):
        q = at.plane_from(d)
        remote(gram.at[q], gram.at[q], h_send.at[d - 1], h_recv.at[q], at.plane(d)[1]).wait_recv()
    w[:, :rank] = gram[...].reshape(rank, rank)
    ids = lax.broadcasted_iota(jnp.int32, (rank, rank), 0)
    lanes = lax.broadcasted_iota(jnp.int32, (rank, rank), 1)
    w[:, rank:] = jnp.where(ids == lanes, 1.0, 0.0).astype(F32)
    b = 64
    steps = rank // b
    later = steps // 2
    moved = 1
    crossed = 0
    for i in range(steps):
        factor_step(w, i * b, b)
        if later <= i + 1 < steps:
            until = F if i + 2 == steps else moved + max(1, (F - 1) // (steps - later))
            for d in range(moved, min(until, F)):
                gathered(d)
            if crossed < moved:
                cross_on(crossed)
                crossed += 1
            moved = min(until, F)
    for i in range(crossed, F):
        cross_on(i)
    inverse = w[:, rank:]
    ortho = dot(whole, inverse, 1, 1)
    left_out[...] = ortho * math.sqrt(rows * F)
    squares = jnp.zeros((1, rank), F32)
    for i in range(F):
        g = at.line_from(i)
        arrive(rd, g)
        v = dot(jnp.concatenate([full[k, g] for k in range(R)], axis=0), inverse, 1, 1)
        squares = squares + jnp.sum(v * v, axis=0, keepdims=True)
        for k in range(R):
            final[k, g] = v[k * piece:(k + 1) * piece]
    sq[...] = jnp.broadcast_to(squares, sq.shape)
    norms = []
    for d in range(1, T):
        copy = remote(sq, sqrecv.at[at.t], s_send.at[d - 1], s_recv.at[at.t], tens[d - 1])
        copy.start()
        norms.append(copy)
    sqrecv[at.t] = sq[...]

    for copy in loads:
        copy.wait()
    o = ortho * -0.1
    for m in range(2):
        here = pl.ds(m * (cols // 2), cols // 2)
        block = jnp.concatenate(
            [final[k, g] for k in range(m * R // 2, (m + 1) * R // 2) for g in range(F)], axis=0
        )
        mom_out[0, :, here] = mom[:, here] + grad[:, here].astype(F32) + dot3(o, block, 1, 1)

    for d in range(1, T):
        k = lax.rem(at.t + T - d, T)
        remote(sq, sqrecv.at[k], s_send.at[d - 1], s_recv.at[k], tens[d - 1]).wait_recv()
    total = sqrecv[0]
    for k in range(1, T):
        total = total + sqrecv[k]
    norm = jnp.sqrt(total[0:1, :] + 1e-06)
    scale = math.sqrt(cols * T) / norm
    for i in range(R):
        k = at.f * R + i
        right_out[i * piece:(i + 1) * piece, :] = final[k // F, lax.rem(k, F)] * scale
    for copy in sent + norms:
        copy.wait_send()


def solution(mesh):
    R, F, T = mesh.shape["replica"], mesh.shape["fsdp"], mesh.shape["tensor"]
    n = R * T
    DMA = pltpu.SemaphoreType.DMA

    def shards(momentum, gradient, right_in):
        rows, cols = momentum.shape[1], momentum.shape[2]
        qb, rank = right_in.shape
        share = cols // R
        nb = F // R
        nc = 8 if qb % 64 == 0 else 1
        piece = share // F
        sds = jax.ShapeDtypeStruct
        slots = lambda m, r: pltpu.VMEM((m, r, rank), F32)
        bmean, proj = pl.pallas_call(
            lambda *refs: project_kernel(R, F, T, *refs),
            out_shape=(sds((rows, share), F32), sds((rows, rank), F32)),
            in_specs=hbm(3),
            out_specs=tuple(vmem(2)),
            scratch_shapes=[
                pltpu.VMEM((rows, cols), F32),
                pltpu.VMEM((rows, cols), gradient.dtype),
                pltpu.VMEM((R, 2, rows * share // 256, 128), F32),
                pltpu.VMEM((2, 3, rows * share // 256, 128), F32),
                pltpu.VMEM((nb, nc, qb // nc, rank), F32),
                slots(n, rows // n),
                slots(n, rows // n),
                slots(n, rows // n),
                DMA((2,)), DMA((nb, nc)), DMA((2, 3)), DMA((2, 3)),
                DMA((nb, nc)), DMA((nb, nc)), DMA((nb, nc)),
                DMA((n,)), DMA((n,)), DMA((n,)), DMA((n,)),
            ],
            compiler_params=pltpu.CompilerParams(
                collective_id=0, has_side_effects=True, vmem_limit_bytes=60 << 20
            ),
            name="project",
        )(momentum, gradient, right_in)
        left, right, updated = pl.pallas_call(
            lambda *refs: back_kernel(R, F, T, *refs),
            out_shape=(sds((rows, rank), F32), sds((qb, rank), F32), sds(momentum.shape, F32)),
            in_specs=hbm(2) + vmem(2),
            out_specs=tuple(vmem(3)),
            scratch_shapes=[
                pltpu.VMEM((rows, cols), F32),
                pltpu.VMEM((rows, cols), gradient.dtype),
                slots(n, rank // n),
                slots(F, rank // n),
                slots(n, rank // n),
                pltpu.VMEM((rank, 2 * rank), F32),
                slots(F, piece),
                slots(F, piece),
                pltpu.VMEM((R, F, piece, rank), F32),
                pltpu.VMEM((R, F, piece, rank), F32),
                pltpu.VMEM((8, rank), F32),
                slots(T, 8),
                DMA((2,)),
                DMA((F,)), DMA((F,)), DMA((n,)), DMA((n,)),
                DMA((F,)), DMA((F,)), DMA((F,)), DMA((F,)),
                DMA((F, R)), DMA((R, F)), DMA((T,)), DMA((T,)),
            ],
            compiler_params=pltpu.CompilerParams(
                collective_id=1, has_side_effects=True, vmem_limit_bytes=40 << 20
            ),
            name="back",
        )(momentum, gradient, bmean, proj)
        return left, right, updated

    placed = (
        P("replica", "fsdp", "tensor"),
        P("replica", "fsdp", "tensor"),
        P(("tensor", "fsdp"), None),
    )
    return jax.shard_map(
        shards,
        mesh=mesh,
        in_specs=placed,
        out_specs=(P("fsdp", None), P(("tensor", "fsdp"), None), P("replica", "fsdp", "tensor")),
        check_vma=False,
    )
```

```python
import math

import jax
import jax.numpy as jnp
from jax import lax
from jax.experimental import pallas as pl
from jax.experimental.pallas import tpu as pltpu
from jax.sharding import PartitionSpec as P

MESH = pl.DeviceIdType.MESH
HIGHEST = lax.Precision.HIGHEST
F32 = jnp.float32


def dot(a, b, ca, cb):
    return lax.dot_general(
        a, b, (((ca,), (cb,)), ((), ())), precision=HIGHEST, preferred_element_type=F32
    )


def halves(a):
    high = a.astype(jnp.bfloat16)
    return high, (a - high.astype(F32)).astype(jnp.bfloat16)


def dot3(a, b, ca, cb):
    ah, al = halves(a)
    bh, bl = halves(b)
    one = lambda x, y: lax.dot_general(x, y, (((ca,), (cb,)), ((), ())), preferred_element_type=F32)
    return one(ah, bh) + (one(ah, bl) + one(al, bh))


def vmem(n):
    return [pl.BlockSpec(memory_space=pltpu.VMEM)] * n


def hbm(n):
    return [pl.BlockSpec(memory_space=pltpu.HBM)] * n


class Place:
    def __init__(self, R, F, T):
        self.R, self.F, self.T, self.n = R, F, T, R * T
        self.r = lax.axis_index("replica")
        self.f = lax.axis_index("fsdp")
        self.t = lax.axis_index("tensor")
        self.p = self.r * T + self.t

    def plane(self, d):
        q = lax.rem(self.p + d, self.n)
        return q, {"replica": q // self.T, "tensor": lax.rem(q, self.T)}

    def plane_from(self, d):
        return lax.rem(self.p + self.n - d, self.n)

    def line(self, d):
        q = lax.rem(self.f + d, self.F)
        return q, {"fsdp": q}

    def line_from(self, d):
        return lax.rem(self.f + self.F - d, self.F)

    def cross(self):
        low = lax.rem(self.r, 2)
        return self.r + 1 - 2 * low, lax.rem(self.r + 2, 4), 3 - self.r

    def rep(self, d):
        q = lax.rem(self.r + d, self.R)
        return q, {"replica": q}

    def rep_from(self, d):
        return lax.rem(self.r + self.R - d, self.R)


def remote(src, dst, send, recv, where):
    return pltpu.make_async_remote_copy(
        src_ref=src, dst_ref=dst, send_sem=send, recv_sem=recv, device_id=where, device_id_type=MESH
    )


def greet(targets):
    barrier = pltpu.get_barrier_semaphore()
    for where in targets:
        pl.semaphore_signal(barrier, inc=1, device_id=where, device_id_type=MESH)
    pl.semaphore_wait(barrier, len(targets))


def pack(part):
    rows, share = part.shape
    whole = share // 128 * 128
    tiles = [part[:, i:i + 128] for i in range(0, whole, 128)]
    if whole < share:
        half = rows // 2
        tiles.append(jnp.concatenate([part[:half, whole:], part[half:, whole:]], axis=1))
    return jnp.concatenate(tiles, axis=0)


def unpack(flat, rows, share):
    whole = share // 128 * 128
    tiles = [flat[i * rows:(i + 1) * rows] for i in range(whole // 128)]
    if whole < share:
        last = flat[whole // 128 * rows:]
        tiles.append(jnp.concatenate([last[:, :64], last[:, 64:]], axis=0))
    return jnp.concatenate(tiles, axis=1)


def project_kernel(
    R, F, T, mom_in, grad_in, q_in, bmean_out, proj_out,
    mom, grad, bufs, brecv, qs, pp, precv, proj,
    in_sem, q_sem, b_send, b_recv, q_up, q_down, q_recv, p_send, p_recv, a_send, a_recv,
):
    at = Place(R, F, T)
    rows, cols = mom.shape
    share = cols // R
    n = at.n
    loads = [
        pltpu.make_async_copy(mom_in.at[0], mom, in_sem.at[0]),
        pltpu.make_async_copy(grad_in.at[0], grad, in_sem.at[1]),
    ]
    for copy in loads:
        copy.start()
    nb = F // R
    nc, qc = qs.shape[1], qs.shape[2]

    def fetch(j, c):
        return pltpu.make_async_copy(q_in.at[pl.ds(c * qc, qc)], qs.at[j, c], q_sem.at[j, c])

    for j in range(nb):
        @pl.when(at.f == at.r * nb + j)
        def _():
            for c in range(nc):
                fetch(j, c).start()

    greet([at.plane(d)[1] for d in range(1, n)] + [at.line(d)[1] for d in range(1, F)])

    for copy in loads:
        copy.wait()
    half = bufs.shape[2]
    for k in range(R):
        part = slice(k * share, (k + 1) * share)
        flat = pack(mom[:, part] + grad[:, part].astype(F32))
        for h in range(2):
            bufs[k, h] = flat[h * half:(h + 1) * half]

    rx, ry, rd = at.cross()
    sent = []

    def hop(src, h, slot, k):
        return remote(bufs.at[src, h], brecv.at[h, slot], b_send.at[h, slot], b_recv.at[h, slot], {"replica": k})

    for slot in range(2):
        for h, first in enumerate((rx, ry)):
            copy = hop((rd, first)[slot], h, slot, first)
            copy.start()
            sent.append(copy)

    def up(j, c):
        return remote(qs.at[j, c], qs.at[j, c], q_up.at[j, c], q_recv.at[j, c], {"fsdp": lax.rem(at.f + 1, F)})

    def down(j, c):
        return remote(qs.at[j, c], qs.at[j, c], q_down.at[j, c], q_recv.at[j, c], {"fsdp": lax.rem(at.f + F - 1, F)})

    def pass_on(c, j):
        home = at.r * nb + j
        @pl.when(at.f == home)
        def _():
            fetch(j, c).wait()
        @pl.when(at.f != home)
        def _():
            up(j, c).wait_recv()
        @pl.when((at.f >= home) & (at.f < F - 1))
        def _():
            up(j, c).start()
        @pl.when((at.f <= home) & (at.f > 0))
        def _():
            down(j, c).start()

    for c in range(nc):
        for j in range(nb):
            pass_on(c, j)
        if c == 0:
            for h, second in enumerate((ry, rx)):
                hop(rd, h, 0, second).wait_recv()
                bufs[second, h] = bufs[second, h] + brecv[h, 0]
                copy = hop(second, h, 2, second)
                copy.start()
                sent.append(copy)
    for h, (first, second) in enumerate(((rx, ry), (ry, rx))):
        hop(first, h, 1, first).wait_recv()
    for h, second in enumerate((ry, rx)):
        hop(second, h, 2, second).wait_recv()
    flat = jnp.concatenate([bufs[at.r, h] + brecv[h, 1] + brecv[h, 2] for h in range(2)], axis=0)
    bmean = unpack(flat * (1.0 / R), rows, share)
    bmean_out[...] = bmean
    part = dot(bmean, qs[...].reshape(share, q_in.shape[1]), 1, 0)
    pp[...] = part.reshape(pp.shape)

    for d in range(1, n):
        q, where = at.plane(d)
        copy = remote(pp.at[q], precv.at[at.p], p_send.at[d - 1], p_recv.at[at.p], where)
        copy.start()
        sent.append(copy)
    precv[at.p] = pp[at.p]
    for d in range(1, n):
        q = at.plane_from(d)
        remote(pp.at[q], precv.at[q], p_send.at[d - 1], p_recv.at[q], at.plane(d)[1]).wait_recv()
    total = precv[0]
    for k in range(1, n):
        total = total + precv[k]
    proj[at.p] = total
    for d in range(1, n):
        q, where = at.plane(d)
        copy = remote(proj.at[at.p], proj.at[at.p], a_send.at[d - 1], a_recv.at[at.p], where)
        copy.start()
        sent.append(copy)
    for d in range(1, n):
        q = at.plane_from(d)
        remote(proj.at[q], proj.at[q], a_send.at[d - 1], a_recv.at[q], at.plane(d)[1]).wait_recv()
    whole = proj[...].reshape(rows, q_in.shape[1])
    proj_out[...] = whole

    for copy in sent:
        copy.wait_send()
    for c in range(nc):
        for j in range(nb):
            home = at.r * nb + j
            @pl.when((at.f >= home) & (at.f < F - 1))
            def _():
                up(j, c).wait_send()
            @pl.when((at.f <= home) & (at.f > 0))
            def _():
                down(j, c).wait_send()


def eliminate(tile, side):
    b = tile.shape[0]
    rows_id = lax.broadcasted_iota(jnp.int32, tile.shape, 0)
    lanes = lax.broadcasted_iota(jnp.int32, tile.shape, 1)
    other = b - side
    inside = (lanes >= side) & (lanes < side + b)
    x = jnp.where(inside, tile, jnp.where(lanes - other == rows_id, 1.0, 0.0).astype(F32))
    done = []
    for k0 in range(0, b, 8):
        shape = x.shape
        ids = lax.broadcasted_iota(jnp.int32, shape, 0)
        panel = [
            jnp.broadcast_to(x[:, side + k0 + j:side + k0 + j + 1], shape) for j in range(8)
        ]
        for j in range(8):
            inverse = 1.0 / panel[j][j:j + 1, :]
            scale = jnp.where(ids > j, panel[j], 0.0) * inverse
            for i in range(j + 1, 8):
                panel[i] = panel[i] - scale * panel[i][j:j + 1, :]
            x = x - scale * x[j:j + 1, :]
        done.append(x[:8])
        x = x[8:]
    x = jnp.concatenate(done, axis=0)
    pivot = jnp.sum(jnp.where(lanes - side == rows_id, x, 0.0), axis=1, keepdims=True)
    return x * (1.0 / jnp.sqrt(pivot))


def factor_step(w, o, b):
    size = w.shape[0]
    base = o // 128 * 128
    side = o - base
    x = eliminate(w[o:o + b, base:base + 128], side)
    block = w[o:o + b, :]
    zero = jnp.zeros_like(block)
    stack = jnp.concatenate([zero, block] if side == 0 else [block, zero], axis=0)
    strip = dot(x, stack, 1, 0)
    w[o:o + b, :] = strip
    if o + b < size:
        update = dot(strip[:, :size], strip, 0, 0)
        w[o + b:, :] = w[o + b:, :] - update[o + b:, :]


def back_kernel(
    R, F, T, mom_in, grad_in, bmean, proj, left_out, right_out, mom_out,
    mom, grad, gp, grecv, gram, w, bp, zrecv, full, final, sq, sqrecv,
    in_sem, g_send, g_recv, h_send, h_recv,
    z_send, z_recv, a_send, a_recv, r_send, r_recv, s_send, s_recv,
):
    at = Place(R, F, T)
    n = at.n
    loads = [
        pltpu.make_async_copy(mom_in.at[0], mom, in_sem.at[0]),
        pltpu.make_async_copy(grad_in.at[0], grad, in_sem.at[1]),
    ]
    for copy in loads:
        copy.start()
    rows, cols = mom.shape
    piece = bp.shape[1]
    rank = proj.shape[1]
    tens = [{"tensor": lax.rem(at.t + d, T)} for d in range(1, T)]
    sent = []

    def go(copy):
        copy.start()
        sent.append(copy)

    rx, ry, rd = at.cross()
    whole = proj[...]
    gp[...] = dot(whole, whole, 0, 0).reshape(gp.shape)
    back = dot(bmean[...], whole, 0, 0)
    for g in range(F):
        bp[g] = back[g * piece:(g + 1) * piece, :]
    greet([at.plane(d)[1] for d in range(1, n)] + [at.line(d)[1] for d in range(1, F)])
    for d in range(1, F):
        q, where = at.line(d)
        go(remote(gp.at[at.p], grecv.at[at.f], g_send.at[d - 1], g_recv.at[at.f], where))
    grecv[at.f] = gp[at.p]

    for d in range(1, F):
        q, where = at.line(d)
        go(remote(bp.at[q], zrecv.at[at.f], z_send.at[d - 1], z_recv.at[at.f], where))
    zrecv[at.f] = bp[at.f]

    for d in range(1, F):
        q = at.line_from(d)
        remote(gp.at[at.p], grecv.at[q], g_send.at[d - 1], g_recv.at[q], at.line(d)[1]).wait_recv()
    total = grecv[0]
    for k in range(1, F):
        total = total + grecv[k]
    gram[at.p] = total
    for d in range(1, n):
        q, where = at.plane(d)
        go(remote(gram.at[at.p], gram.at[at.p], h_send.at[d - 1], h_recv.at[at.p], where))

    def forward(f, i):
        slot = full.at[at.r, f]
        for e, k in enumerate((rx, ry)):
            go(remote(slot, slot, r_send.at[i, e], r_recv.at[at.r, f], {"replica": k}))

    def arrive(k, g):
        slot = full.at[k, g]
        remote(slot, slot, r_send.at[0, 0], r_recv.at[k, g], {"replica": rx}).wait_recv()

    def cross_on(i):
        g = at.line_from(i)
        arrive(rx, g)
        arrive(ry, g)
        odd = lax.rem(g, 2)
        src = rx + (ry - rx) * odd
        slot = full.at[src, g]
        go(remote(slot, slot, r_send.at[i, 2], r_recv.at[src, g], {"replica": ry + (rx - ry) * odd}))

    def reduced():
        for d in range(1, F):
            q = at.line_from(d)
            remote(bp.at[q], zrecv.at[q], z_send.at[d - 1], z_recv.at[q], at.line(d)[1]).wait_recv()
        total = zrecv[0]
        for k in range(1, F):
            total = total + zrecv[k]
        full[at.r, at.f] = total
        for d in range(1, F):
            q, where = at.line(d)
            go(remote(full.at[at.r, at.f], full.at[at.r, at.f], a_send.at[d - 1], a_recv.at[at.f], where))
        forward(at.f, 0)

    def gathered(d):
        q = at.line_from(d)
        remote(full.at[at.r, q], full.at[at.r, q], a_send.at[d - 1], a_recv.at[q], at.line(d)[1]).wait_recv()
        forward(q, d)

    reduced()
    for d in range(1, n):
        q = at.plane_from(d)
        remote(gram.at[q], gram.at[q], h_send.at[d - 1], h_recv.at[q], at.plane(d)[1]).wait_recv()
    w[:, :rank] = gram[...].reshape(rank, rank)
    ids = lax.broadcasted_iota(jnp.int32, (rank, rank), 0)
    lanes = lax.broadcasted_iota(jnp.int32, (rank, rank), 1)
    w[:, rank:] = jnp.where(ids == lanes, 1.0, 0.0).astype(F32)
    b = 64
    steps = rank // b
    later = 1
    moved = 1
    crossed = 0
    for i in range(steps):
        factor_step(w, i * b, b)
        if later <= i + 1 < steps:
            until = F if i + 2 == steps else moved + max(1, (F - 1) // (steps - later))
            for d in range(moved, min(until, F)):
                gathered(d)
            if crossed < moved:
                cross_on(crossed)
                crossed += 1
            moved = min(until, F)
    for i in range(crossed, F):
        cross_on(i)
    inverse = w[:, rank:]
    ortho = dot(whole, inverse, 1, 1)
    left_out[...] = ortho * math.sqrt(rows * F)
    squares = jnp.zeros((1, rank), F32)
    for i in range(F):
        g = at.line_from(i)
        arrive(rd, g)
        v = dot(jnp.concatenate([full[k, g] for k in range(R)], axis=0), inverse, 1, 1)
        squares = squares + jnp.sum(v * v, axis=0, keepdims=True)
        for k in range(R):
            final[k, g] = v[k * piece:(k + 1) * piece]
    sq[...] = jnp.broadcast_to(squares, sq.shape)
    norms = []
    for d in range(1, T):
        copy = remote(sq, sqrecv.at[at.t], s_send.at[d - 1], s_recv.at[at.t], tens[d - 1])
        copy.start()
        norms.append(copy)
    sqrecv[at.t] = sq[...]

    for copy in loads:
        copy.wait()
    o = ortho * -0.1
    for m in range(2):
        here = pl.ds(m * (cols // 2), cols // 2)
        block = jnp.concatenate(
            [final[k, g] for k in range(m * R // 2, (m + 1) * R // 2) for g in range(F)], axis=0
        )
        mom_out[0, :, here] = mom[:, here] + grad[:, here].astype(F32) + dot3(o, block, 1, 1)

    for d in range(1, T):
        k = lax.rem(at.t + T - d, T)
        remote(sq, sqrecv.at[k], s_send.at[d - 1], s_recv.at[k], tens[d - 1]).wait_recv()
    total = sqrecv[0]
    for k in range(1, T):
        total = total + sqrecv[k]
    norm = jnp.sqrt(total[0:1, :] + 1e-06)
    scale = math.sqrt(cols * T) / norm
    for i in range(R):
        k = at.f * R + i
        right_out[i * piece:(i + 1) * piece, :] = final[k // F, lax.rem(k, F)] * scale
    for copy in sent + norms:
        copy.wait_send()


def solution(mesh):
    R, F, T = mesh.shape["replica"], mesh.shape["fsdp"], mesh.shape["tensor"]
    n = R * T
    DMA = pltpu.SemaphoreType.DMA

    def shards(momentum, gradient, right_in):
        rows, cols = momentum.shape[1], momentum.shape[2]
        qb, rank = right_in.shape
        share = cols // R
        nb = F // R
        nc = 8 if qb % 64 == 0 else 1
        piece = share // F
        sds = jax.ShapeDtypeStruct
        slots = lambda m, r: pltpu.VMEM((m, r, rank), F32)
        bmean, proj = pl.pallas_call(
            lambda *refs: project_kernel(R, F, T, *refs),
            out_shape=(sds((rows, share), F32), sds((rows, rank), F32)),
            in_specs=hbm(3),
            out_specs=tuple(vmem(2)),
            scratch_shapes=[
                pltpu.VMEM((rows, cols), F32),
                pltpu.VMEM((rows, cols), gradient.dtype),
                pltpu.VMEM((R, 2, rows * share // 256, 128), F32),
                pltpu.VMEM((2, 3, rows * share // 256, 128), F32),
                pltpu.VMEM((nb, nc, qb // nc, rank), F32),
                slots(n, rows // n),
                slots(n, rows // n),
                slots(n, rows // n),
                DMA((2,)), DMA((nb, nc)), DMA((2, 3)), DMA((2, 3)),
                DMA((nb, nc)), DMA((nb, nc)), DMA((nb, nc)),
                DMA((n,)), DMA((n,)), DMA((n,)), DMA((n,)),
            ],
            compiler_params=pltpu.CompilerParams(
                collective_id=0, has_side_effects=True, vmem_limit_bytes=60 << 20
            ),
            name="project",
        )(momentum, gradient, right_in)
        left, right, updated = pl.pallas_call(
            lambda *refs: back_kernel(R, F, T, *refs),
            out_shape=(sds((rows, rank), F32), sds((qb, rank), F32), sds(momentum.shape, F32)),
            in_specs=hbm(2) + vmem(2),
            out_specs=tuple(vmem(3)),
            scratch_shapes=[
                pltpu.VMEM((rows, cols), F32),
                pltpu.VMEM((rows, cols), gradient.dtype),
                slots(n, rank // n),
                slots(F, rank // n),
                slots(n, rank // n),
                pltpu.VMEM((rank, 2 * rank), F32),
                slots(F, piece),
                slots(F, piece),
                pltpu.VMEM((R, F, piece, rank), F32),
                pltpu.VMEM((R, F, piece, rank), F32),
                pltpu.VMEM((8, rank), F32),
                slots(T, 8),
                DMA((2,)),
                DMA((F,)), DMA((F,)), DMA((n,)), DMA((n,)),
                DMA((F,)), DMA((F,)), DMA((F,)), DMA((F,)),
                DMA((F, R)), DMA((R, F)), DMA((T,)), DMA((T,)),
            ],
            compiler_params=pltpu.CompilerParams(
                collective_id=1, has_side_effects=True, vmem_limit_bytes=40 << 20
            ),
            name="back",
        )(momentum, gradient, bmean, proj)
        return left, right, updated

    placed = (
        P("replica", "fsdp", "tensor"),
        P("replica", "fsdp", "tensor"),
        P(("tensor", "fsdp"), None),
    )
    return jax.shard_map(
        shards,
        mesh=mesh,
        in_specs=placed,
        out_specs=(P("fsdp", None), P(("tensor", "fsdp"), None), P("replica", "fsdp", "tensor")),
        check_vma=False,
    )
```
